256 devices in a mesh: table: 128 (over y, z, x), row: 2 (over core).
Axes of the slice: x: 4, y: 4, z: 8, core: 2. Of those that a mesh axis runs over, the one named last changes fastest.
Arguments:
- dense_input: bfloat16 [4096, 13], P(('table', 'row')), may hold values from -6 to 6
- bottom_first: bfloat16 [13, 512], replicated, may hold values from -1.75 to 1.75
- bottom_second: bfloat16 [512, 256], replicated, may hold values from -0.375 to 0.375
- bottom_third: bfloat16 [256, 128], replicated, may hold values from -0.5 to 0.5
- wide_tables: bfloat16 [1048576, 256], P(('table', 'row')), may hold values from -6 to 6
- narrow_tables: bfloat16 [1048576, 64], P(('table', 'row')), may hold values from -6 to 6
- wide_indices: int32 [4096, 32, 8], P(('table', 'row')), may hold values from 0 to 32767
- wide_lengths: int32 [4096, 32], P(('table', 'row')), may hold values from 4 to 8
- narrow_indices: int32 [4096, 32, 8], P(('table', 'row')), may hold values from 0 to 32767
- narrow_lengths: int32 [4096, 32], P(('table', 'row')), may hold values from 4 to 8
- wide_projection: bfloat16 [32, 256, 128], replicated, may hold values from -0.125 to 0.125
- narrow_projection: bfloat16 [32, 64, 128], replicated, may hold values from -0.25 to 0.25
- top_first: bfloat16 [2208, 1024], replicated, may hold values from -0.0234375 to 0.0234375
- top_last: bfloat16 [1024], replicated, may hold values from -0.1875 to 0.1875
Outputs:
- hidden: bfloat16 [4096, 1024], P(('table', 'row'))
- logits: float32 [4096], P(('table', 'row'))
The draws below stay inside these ranges and needn't reach their ends.
All inputs are finite; a program needn't handle non-finite values.
Results may differ from the reference program's by a relative error of at most 0.02.
Values may be sent and summed in bfloat16 or wider, within the bound.
No kernel may reach another device: no remote copies, remote signals or barrier semaphores. Data moves between devices by JAX's collectives and lax.ppermute only.
A program may use at most 64 MiB of HBM per device.

```python
import jax
import jax.numpy as jnp
import numpy as np
from jax import lax

WW = 256
WN = 64
EMB = 128
DENSE_IN = 13
BOT1 = 512
BOT2 = 256
TOP = 1024
POOL = 8
R_DEV = 4096
TW = 32
TN = 32
BATCH = 4096
TABLE_ROWS = 32768
FEATURES = 65
INTER = 2208


def full_choice(key, table_total, salt):
    return jax.random.randint(jax.random.fold_in(key, salt), (), 0, table_total)


def drawn_rows(key, table_total, salt):
    shard_total = TABLE_ROWS // R_DEV
    full_table = full_choice(key, table_total, salt)
    score_key = jax.random.fold_in(key, salt + 1)
    loose_key = jax.random.fold_in(key, salt + 2)
    pick_key = jax.random.fold_in(key, salt + 3)
    offset_key = jax.random.fold_in(key, salt + 4)
    scores = jax.random.randint(score_key, (BATCH, table_total, shard_total), 0, 1 << 20) * shard_total + jnp.arange(shard_total, dtype=jnp.int32)
    distinct = jnp.argsort(scores, axis=-1)[..., :POOL].astype(jnp.int32)
    loose = jax.random.randint(loose_key, (BATCH, table_total, POOL), 0, shard_total)
    scattered = jax.random.randint(pick_key, (BATCH, table_total, 1), 0, 4) == 0
    scattered = scattered & (jnp.arange(table_total)[None, :, None] != full_table)
    shards = jnp.where(scattered, loose, distinct)
    offsets = jax.random.randint(offset_key, (BATCH, table_total, POOL), 0, R_DEV)
    return (shards * R_DEV + offsets).astype(jnp.int32)


def drawn_lengths(key, table_total, salt):
    full_table = full_choice(key, table_total, salt)
    drawn = jax.random.randint(jax.random.fold_in(key, salt + 5), (BATCH, table_total), POOL // 2, POOL + 1)
    return jnp.where(jnp.arange(table_total)[None, :] == full_table, POOL, drawn).astype(jnp.int32)


def draw_wide_indices(key, part):
    return drawn_rows(key, TW, 11)


def draw_wide_lengths(key, part):
    return drawn_lengths(key, TW, 11)


def draw_narrow_indices(key, part):
    return drawn_rows(key, TN, 31)


def draw_narrow_lengths(key, part):
    return drawn_lengths(key, TN, 31)


def block_levels(own_key, extent, split, least, largest):
    level, own = 1.0, jax.random.fold_in(own_key, 6)
    for axis_at, shards_of in split:
        steps = jnp.exp(jax.random.uniform(jax.random.fold_in(own, axis_at), (shards_of,), jnp.float32, least / len(split), largest / len(split)))
        level = level * jnp.repeat(steps, extent[axis_at] // shards_of).reshape([-1 if axis == axis_at else 1 for axis in range(len(extent))])
    return level


def scatter_about(key, dims, scale, limit, cuts=(), kind=jnp.bfloat16):
    level = block_levels(key, dims, cuts, -0.22, 0.18) if cuts else 1.0
    values = jax.random.normal(key, dims, jnp.float32) * scale * level
    return jnp.minimum(jnp.maximum(values, -limit), limit).astype(kind)


def setup_inputs(seed: int = 0) -> dict:
    keys = jax.random.split(jax.random.key(seed), 15)
    dense_input = scatter_about(keys[0], (BATCH, DENSE_IN), 1.0, 6.0, ((0, 256),))
    bottom_first = scatter_about(keys[1], (DENSE_IN, BOT1), DENSE_IN ** -0.5, 1.75)
    bottom_second = scatter_about(keys[2], (BOT1, BOT2), (BOT1 // 2) ** -0.5, 0.375)
    bottom_third = scatter_about(keys[3], (BOT2, EMB), (BOT2 // 2) ** -0.5, 0.5)
    wide_tables = scatter_about(keys[4], (TW * TABLE_ROWS, WW), 1.0, 6.0, ((0, 256),))
    narrow_tables = scatter_about(keys[5], (TN * TABLE_ROWS, WN), 1.0, 6.0, ((0, 256),))
    wide_indices = draw_wide_indices(jax.random.fold_in(keys[14], 71), 0)
    wide_lengths = draw_wide_lengths(jax.random.fold_in(keys[14], 71), 0)
    narrow_indices = draw_narrow_indices(jax.random.fold_in(keys[14], 71), 0)
    narrow_lengths = draw_narrow_lengths(jax.random.fold_in(keys[14], 71), 0)
    wide_projection = scatter_about(keys[10], (TW, WW, EMB), (8 * WW) ** -0.5, 0.125)
    narrow_projection = scatter_about(keys[11], (TN, WN, EMB), (8 * WN) ** -0.5, 0.25)
    top_first = scatter_about(keys[12], (INTER, TOP), (32 * INTER) ** -0.5, 0.0234375)
    top_last = scatter_about(keys[13], (TOP,), TOP ** -0.5, 0.1875)
    return {"dense_input": dense_input, "bottom_first": bottom_first, "bottom_second": bottom_second, "bottom_third": bottom_third, "wide_tables": wide_tables, "narrow_tables": narrow_tables, "wide_indices": wide_indices, "wide_lengths": wide_lengths, "narrow_indices": narrow_indices, "narrow_lengths": narrow_lengths, "wide_projection": wide_projection, "narrow_projection": narrow_projection, "top_first": top_first, "top_last": top_last}


def dense_layer(values, weight):
    return jnp.maximum(jnp.dot(values, weight, preferred_element_type=jnp.float32), 0.0).astype(jnp.bfloat16)


def pool_tables(table_rows, indices, lengths, table_total):
    tables = table_rows.reshape(table_total, table_rows.shape[0] // table_total, table_rows.shape[1])

    def one_table(operands):
        table_now, bag_ids, bag_sizes = operands
        summed = jnp.zeros((bag_ids.shape[0], table_now.shape[1]), jnp.float32)
        for slot_pos in range(bag_ids.shape[1]):
            looked_up = jnp.take(table_now, bag_ids[:, slot_pos], axis=0).astype(jnp.float32)
            summed = summed + jnp.where((bag_sizes > slot_pos)[:, None], looked_up, 0.0)
        return summed

    return lax.map(one_table, (tables, jnp.swapaxes(indices, 0, 1), jnp.swapaxes(lengths, 0, 1)))


def reference(dense_input, bottom_first, bottom_second, bottom_third, wide_tables, narrow_tables, wide_indices, wide_lengths, narrow_indices, narrow_lengths, wide_projection, narrow_projection, top_first, top_last):
    bottom = dense_layer(dense_layer(dense_layer(dense_input, bottom_first), bottom_second), bottom_third)
    wide_pooled = pool_tables(wide_tables, wide_indices, wide_lengths, TW)
    wide_embedded = jnp.einsum("tbw,twe->tbe", wide_pooled, wide_projection.astype(jnp.float32), precision=lax.Precision.HIGHEST).astype(jnp.bfloat16)
    narrow_pooled = pool_tables(narrow_tables, narrow_indices, narrow_lengths, TN).astype(jnp.bfloat16)
    narrow_embedded = jnp.einsum("tbw,twe->tbe", narrow_pooled.astype(jnp.float32), narrow_projection.astype(jnp.float32), precision=lax.Precision.HIGHEST).astype(jnp.bfloat16)
    features = jnp.concatenate([bottom[None], wide_embedded, narrow_embedded], 0).astype(jnp.float32)
    products = jnp.einsum("fbe,gbe->bfg", features, features, precision=lax.Precision.HIGHEST)
    first_side, second_side = np.triu_indices(FEATURES, 1)
    pair_values = products[:, first_side, second_side]
    joined = jnp.concatenate([bottom.astype(jnp.float32), pair_values], 1).astype(jnp.bfloat16)
    hidden = dense_layer(joined, top_first)
    logits = jnp.dot(hidden, top_last, preferred_element_type=jnp.float32)
    return hidden, logits
```

```python
import jax
import jax.numpy as jnp
from jax import lax
from jax.experimental import pallas as pl
from jax.experimental.pallas import tpu as pltpu
from jax.sharding import Mesh
from jax.sharding import PartitionSpec as P

SLOTS = 8
BAGS = 16
LANES = 128


def entries(value, shard, lane):
    local = (value >> 12) == shard
    ones = local.astype(jnp.int32)
    run = ones
    for step in (16, 32, 64):
        run = run + jnp.where(lane >= step, pltpu.roll(run, step, 1), 0)
    rank = run - ones
    gap = (lane >> 4) - rank
    packed = jnp.where(local, (value & 4095) | (gap << 16) | (1 << 24), 0)
    for bit in (0, 1, 2):
        moved = jnp.where((packed & (1 << (16 + bit))) != 0, packed, 0)
        packed = packed - moved + pltpu.roll(moved, LANES - (16 << bit), 1)
    first = jnp.where(packed != 0, packed & 4095, 4096)
    more = (packed != 0) & (lane >= BAGS)
    ones = more.astype(jnp.int32)
    run = ones
    for step in (1, 2, 4, 8, 16, 32, 64):
        run = run + jnp.where(lane >= step, pltpu.roll(run, step, 1), 0)
    gap = lane - (run - ones)
    extra = jnp.where(more, (packed & 4095) | ((lane & 15) << 12) | (gap << 16) | (1 << 24), 0)
    for bit in range(7):
        moved = jnp.where((extra & (1 << (16 + bit))) != 0, extra, 0)
        extra = extra - moved + pltpu.roll(moved, LANES - (1 << bit), 1)
    return first, jnp.where(lane == LANES - 1, run, extra & 65535)


def pool_kernel(place_ref, words_ref, wide_ref, narrow_ref, keep_ref, send_ref,
                wide_rows, narrow_rows, wide_sum, narrow_sum, firsts_v, wmore_v, nmore_v,
                firsts, wmore, nmore, sems):
    copies = [
        pltpu.make_async_copy(wide_ref, wide_rows.at[pl.ds(0, 4096)], sems.at[0]),
        pltpu.make_async_copy(narrow_ref, narrow_rows.at[pl.ds(0, 4096)], sems.at[1]),
    ]
    for copy in copies:
        copy.start()
    my_x = place_ref[0]
    my_row = place_ref[1]
    shard = my_x * 2 + my_row
    wide_rows[pl.ds(4096, 8), :] = jnp.zeros((8, LANES), jnp.float32)
    narrow_rows[pl.ds(4096, 8), :] = jnp.zeros((8, LANES), jnp.float32)
    lane = lax.broadcasted_iota(jnp.int32, (32, LANES), 1)

    def prepare(j, total):
        rows = pl.ds(pl.multiple_of(j * 32, 32), 32)
        words = words_ref[rows, :]
        wfirst, wlist = entries(words & 65535, shard, lane)
        nfirst, nlist = entries((words >> 16) & 65535, shard, lane)
        wmore_v[rows, :] = wlist
        nmore_v[rows, :] = nlist
        pair = jnp.where(lane < BAGS, wfirst | (nfirst << 16), 0)
        return total + pltpu.roll(pair, j * BAGS, 1)

    firsts_v[...] = lax.fori_loop(0, 8, prepare, jnp.zeros((32, LANES), jnp.int32))
    lists = [
        pltpu.make_async_copy(firsts_v, firsts, sems.at[2]),
        pltpu.make_async_copy(wmore_v, wmore, sems.at[3]),
        pltpu.make_async_copy(nmore_v, nmore, sems.at[4]),
    ]
    for copy in lists:
        copy.start()
    for copy in lists + copies:
        copy.wait()

    def base_of(source):
        yz = source >> 3
        x = (source >> 1) & 3
        row = source & 1
        return ((row ^ my_row) << 11) + (((x - my_x) & 3) << 9) + (yz << 4)

    def one_source(source, _):
        base = pl.multiple_of(base_of(source), BAGS)
        group = source & 31
        column = (source >> 5) * BAGS
        for bag in range(BAGS):
            pair = firsts[group, column + bag]
            wide_sum[pl.ds(base + bag, 1), :] = wide_rows[pl.ds(pair & 65535, 1), :]
            narrow_sum[pl.ds(base + bag, 1), :] = narrow_rows[pl.ds(pair >> 16, 1), :]
        return 0

    lax.fori_loop(0, 256, one_source, 0)

    def more_of(source, _):
        base = base_of(source)

        def add(lists, rows, total):
            def one(i, _):
                entry = lists[source, i]
                at = pl.ds(base + (entry >> 12), 1)
                total[at, :] = total[at, :] + rows[pl.ds(entry & 4095, 1), :]
                return 0

            lax.fori_loop(0, lists[source, LANES - 1], one, 0)

        add(wmore, wide_rows, wide_sum)
        add(nmore, narrow_rows, narrow_sum)
        return 0

    lax.fori_loop(0, 256, more_of, 0)

    def finish(ref, start):
        def one(i, _):
            rows = pl.ds(pl.multiple_of(i * 128, 128), 128)
            source = pl.ds(pl.multiple_of(start + i * 128, 128), 128)
            ref[rows, 0:LANES] = wide_sum[source, :].astype(jnp.bfloat16)
            ref[rows, LANES:] = narrow_sum[source, :].astype(jnp.bfloat16)
            return 0

        lax.fori_loop(0, 16, one, 0)

    finish(keep_ref, 0)
    finish(send_ref, 2048)


def pool(place, words, wide, narrow):
    vmem = pl.BlockSpec(memory_space=pltpu.VMEM)
    half = jax.ShapeDtypeStruct((2048, 256), jnp.bfloat16)
    return pl.pallas_call(
        pool_kernel,
        out_shape=(half, half),
        in_specs=[pl.BlockSpec(memory_space=pltpu.SMEM), vmem,
                  pl.BlockSpec(memory_space=pl.ANY), pl.BlockSpec(memory_space=pl.ANY)],
        out_specs=(vmem, vmem),
        scratch_shapes=[
            pltpu.VMEM((4104, LANES), jnp.float32),
            pltpu.VMEM((4104, LANES), jnp.float32),
            pltpu.VMEM((4096, LANES), jnp.float32),
            pltpu.VMEM((4096, LANES), jnp.float32),
            pltpu.VMEM((32, LANES), jnp.int32),
            pltpu.VMEM((256, LANES), jnp.int32),
            pltpu.VMEM((256, LANES), jnp.int32),
            pltpu.SMEM((32, LANES), jnp.int32),
            pltpu.SMEM((256, LANES), jnp.int32),
            pltpu.SMEM((256, LANES), jnp.int32),
            pltpu.SemaphoreType.DMA((5,)),
        ],
        compiler_params=pltpu.CompilerParams(vmem_limit_bytes=40 * 1024 * 1024),
    )(place, words, wide, narrow)


HOME = ("y", "z", "x", "row")
TABLES = ("y", "z")


def dense_layer(values, weight):
    return jnp.maximum(jnp.dot(values, weight, preferred_element_type=jnp.float32), 0.0).astype(
        jnp.bfloat16
    )


def turned(block, axis, count, shift):
    return lax.ppermute(block, axis, [(i, (i + shift) % count) for i in range(count)])


def coded(indices, lengths):
    slots = lax.broadcasted_iota(jnp.int32, indices.shape, 2)
    return jnp.where(slots < lengths[:, :, None], indices, 32768)


def body(
    dense_input,
    bottom_first,
    bottom_second,
    bottom_third,
    wide_tables,
    narrow_tables,
    wide_indices,
    wide_lengths,
    narrow_indices,
    narrow_lengths,
    wide_projection,
    narrow_projection,
    top_first,
    top_last,
):
    own_table = lax.axis_index(TABLES)
    place = jnp.stack([lax.axis_index("x"), lax.axis_index("row")]).astype(jnp.int32)

    words = coded(wide_indices, wide_lengths) | (coded(narrow_indices, narrow_lengths) << 16)
    words = jnp.transpose(words, (1, 2, 0)).reshape(32, 1, LANES)
    words = jnp.broadcast_to(words, (32, 8, LANES)).reshape(256, LANES)
    words = lax.all_to_all(words, HOME, 0, 0, tiled=True)

    wide_weight = lax.dynamic_index_in_dim(wide_projection, own_table, 0, keepdims=False)
    narrow_weight = lax.dynamic_index_in_dim(narrow_projection, own_table, 0, keepdims=False)
    wide_rows = jnp.dot(wide_tables, wide_weight, preferred_element_type=jnp.float32)
    narrow_rows = jnp.dot(narrow_tables, narrow_weight, preferred_element_type=jnp.float32)

    keep, send = pool(place, words, wide_rows, narrow_rows)
    other = turned(send, "row", 2, 1)
    both = (keep.astype(jnp.float32) + other.astype(jnp.float32)).astype(jnp.bfloat16)
    both = both.reshape(4, 512, 256)
    total = both[0].astype(jnp.float32)
    for shift in (1, 2, 3):
        total = total + turned(both[shift], "x", 4, shift).astype(jnp.float32)
    home = lax.all_to_all(
        total.astype(jnp.bfloat16).reshape(32, BAGS, 256), TABLES, 0, 0, tiled=True
    )

    bottom = dense_layer(
        dense_layer(dense_layer(dense_input, bottom_first), bottom_second), bottom_third
    )
    features = jnp.concatenate([bottom[None], home[:, :, :LANES], home[:, :, LANES:]], 0)
    products = jnp.einsum("fbe,gbe->bfg", features, features, preferred_element_type=jnp.float32)
    pairs = jnp.concatenate([products[:, f, f + 1 :] for f in range(64)], 1)
    joined = jnp.concatenate([bottom.astype(jnp.float32), pairs], 1).astype(jnp.bfloat16)
    hidden = dense_layer(joined, top_first)
    logits = jnp.dot(hidden, top_last, preferred_element_type=jnp.float32)
    return (hidden, logits)


def solution(mesh):
    fine = Mesh(mesh.devices.reshape(4, 8, 4, 2), HOME)
    split = P(HOME)
    in_specs = (split, P(), P(), P()) + (split,) * 6 + (P(),) * 4
    return jax.shard_map(
        body, mesh=fine, in_specs=in_specs, out_specs=(split, split), check_vma=False
    )
```

```python
import jax
import jax.numpy as jnp
from jax import lax
from jax.experimental import pallas as pl
from jax.experimental.pallas import tpu as pltpu
from jax.sharding import Mesh
from jax.sharding import PartitionSpec as P

SLOTS = 8
BAGS = 16
LANES = 128
ROWS = 4096
SOURCES = 256


def drawn_left(packed, field, unit, bits):
    for bit in range(bits):
        moved = jnp.where((packed & (1 << (field + bit))) != 0, packed, 0)
        packed = packed - moved + pltpu.roll(moved, LANES - (unit << bit), 1)
    return packed


def counted(flags, before):
    return jnp.dot(
        jnp.where(flags, 1.0, 0.0).astype(jnp.bfloat16), before, preferred_element_type=jnp.float32
    ).astype(jnp.int32)


def as_matrix(flags):
    return jnp.where(flags, 1.0, 0.0).astype(jnp.bfloat16)


def pool_kernel(place_ref, words_ref, wide_ref, narrow_ref, keep_ref, send_ref,
                wide_rows, narrow_rows, wide_sum, narrow_sum, firsts_v, more_v, lists_v,
                firsts, lists, sems):
    tables = [
        pltpu.make_async_copy(wide_ref, wide_rows.at[pl.ds(0, ROWS)], sems.at[0]),
        pltpu.make_async_copy(narrow_ref, narrow_rows.at[pl.ds(0, ROWS)], sems.at[1]),
    ]
    for copy in tables:
        copy.start()
    my_x = place_ref[0]
    my_row = place_ref[1]
    shard = my_x * 2 + my_row
    wide_rows[pl.ds(ROWS, 8), :] = jnp.zeros((8, LANES), jnp.float32)
    narrow_rows[pl.ds(ROWS, 8), :] = jnp.zeros((8, LANES), jnp.float32)
    at = lax.broadcasted_iota(jnp.int32, (LANES, LANES), 0)
    to = lax.broadcasted_iota(jnp.int32, (LANES, LANES), 1)
    same_bag = as_matrix(((at & 15) == (to & 15)) & (at < to))
    any_bag = as_matrix(at < to)

    def base_of(source):
        yz = source >> 3
        x = (source >> 1) & 3
        row = source & 1
        return ((row ^ my_row) << 11) + (((x - my_x) & 3) << 9) + (yz << 4)

    lane = lax.broadcasted_iota(jnp.int32, (SOURCES, LANES), 1)
    target = base_of(lax.broadcasted_iota(jnp.int32, (SOURCES, LANES), 0)) + (lane & 15)
    words = words_ref[...]
    most = jnp.int32(0)
    picks = []
    for kind, value in enumerate((words & 65535, (words >> 16) & 65535)):
        local = (value >> 12) == shard
        gap = (lane >> 4) - counted(local, same_bag)
        packed = jnp.where(local, (value & 4095) | (gap << 12) | (1 << 15), 0)
        packed = drawn_left(packed, 12, BAGS, 3)
        picks.append(jnp.where(packed != 0, packed & 4095, ROWS))
        more = (packed != 0) & (lane >= BAGS)
        before = counted(more, any_bag)
        most = jnp.maximum(most, jnp.max(before + more.astype(jnp.int32)))
        extra = (packed & 4095) | (target << 12) | ((lane - before) << 24) | jnp.int32(-(2**31))
        extra = drawn_left(jnp.where(more, extra, 0), 24, 1, 7)
        more_v[kind] = jnp.transpose(extra)
    pair = jnp.where(lane < BAGS, picks[0] | (picks[1] << 16), 0)
    line = pair[0:32]
    for j in range(1, 8):
        line = line + pltpu.roll(pair[j * 32 : (j + 1) * 32], j * BAGS, 1)
    firsts_v[...] = line
    first_copy = pltpu.make_async_copy(firsts_v, firsts, sems.at[2])
    first_copy.start()
    first_copy.wait()
    for copy in tables:
        copy.wait()

    def one_group(group, _):
        for j in range(8):
            base = pl.multiple_of(base_of(j * 32 + group), BAGS)
            for low in range(0, BAGS, 8):
                bags = range(low, low + 8)
                both = [firsts[group, j * BAGS + bag] for bag in bags]
                wide = [wide_rows[pl.ds(pair & 65535, 1), :] for pair in both]
                narrow = [narrow_rows[pl.ds(pair >> 16, 1), :] for pair in both]
                for bag, row in zip(bags, wide):
                    wide_sum[pl.ds(base + bag, 1), :] = row
                for bag, row in zip(bags, narrow):
                    narrow_sum[pl.ds(base + bag, 1), :] = row
        return 0

    lax.fori_loop(0, 32, one_group, 0)

    lane32 = lax.broadcasted_iota(jnp.int32, (32, LANES), 1)

    def one_block(block, _):
        rows = pl.ds(pl.multiple_of(block * 8, 8), 8)
        held = jnp.concatenate(
            [more_v[kind, rows, half * LANES : (half + 1) * LANES] for kind in (0, 1) for half in (0, 1)], 0
        )
        used = held < 0
        before = counted(used, any_bag)
        total = jnp.sum(used.astype(jnp.int32), axis=1, keepdims=True)
        packed = jnp.where(used, (held & 0xFFFFFF) | ((lane32 - before) << 24), 0)
        packed = drawn_left(packed, 24, 1, 7) & 0xFFFFFF
        lists_v[...] = packed | jnp.where(lane32 == 0, total << 24, 0)
        copy = pltpu.make_async_copy(lists_v, lists, sems.at[3])
        copy.start()
        copy.wait()

        def add(low, rows, sums):
            def one_list(k, _):
                def some(low, count):
                    entries = [lists[k, low + i] for i in range(count)]
                    places = [pl.ds((entry >> 12) & 4095, 1) for entry in entries]
                    values = [
                        sums[place, :] + rows[pl.ds(entry & 4095, 1), :]
                        for entry, place in zip(entries, places)
                    ]
                    for place, value in zip(places, values):
                        sums[place, :] = value

                def four(i, _):
                    some(i * 4, 4)
                    return 0

                def one(i, _):
                    some(i, 1)
                    return 0

                count = lax.shift_right_logical(lists[k, 0], 24)
                lax.fori_loop(0, count // 4, four, 0)
                lax.fori_loop(count // 4 * 4, count, one, 0)
                return 0

            lax.fori_loop(low, low + 16, one_list, 0)

        add(0, wide_rows, wide_sum)
        add(16, narrow_rows, narrow_sum)
        return 0

    lax.fori_loop(0, (most + 7) >> 3, one_block, 0)

    def finish(ref, start):
        def one(i, _):
            rows = pl.ds(pl.multiple_of(i * 128, 128), 128)
            source = pl.ds(pl.multiple_of(start + i * 128, 128), 128)
            ref[rows, 0:LANES] = wide_sum[source, :].astype(jnp.bfloat16)
            ref[rows, LANES:] = narrow_sum[source, :].astype(jnp.bfloat16)
            return 0

        lax.fori_loop(0, 16, one, 0)

    finish(keep_ref, 0)
    finish(send_ref, 2048)


def pool(place, words, wide, narrow):
    vmem = pl.BlockSpec(memory_space=pltpu.VMEM)
    half = jax.ShapeDtypeStruct((2048, 256), jnp.bfloat16)
    return pl.pallas_call(
        pool_kernel,
        out_shape=(half, half),
        in_specs=[pl.BlockSpec(memory_space=pltpu.SMEM), vmem,
                  pl.BlockSpec(memory_space=pl.ANY), pl.BlockSpec(memory_space=pl.ANY)],
        out_specs=(vmem, vmem),
        scratch_shapes=[
            pltpu.VMEM((ROWS + 8, LANES), jnp.float32),
            pltpu.VMEM((ROWS + 8, LANES), jnp.float32),
            pltpu.VMEM((ROWS, LANES), jnp.float32),
            pltpu.VMEM((ROWS, LANES), jnp.float32),
            pltpu.VMEM((32, LANES), jnp.int32),
            pltpu.VMEM((2, LANES, SOURCES), jnp.int32),
            pltpu.VMEM((32, LANES), jnp.int32),
            pltpu.SMEM((32, LANES), jnp.int32),
            pltpu.SMEM((32, LANES), jnp.int32),
            pltpu.SemaphoreType.DMA((4,)),
        ],
        compiler_params=pltpu.CompilerParams(vmem_limit_bytes=60 * 1024 * 1024),
    )(place, words, wide, narrow)


HOME = ("y", "z", "x", "row")
TABLES = ("y", "z")


def dense_layer(values, weight):
    return jnp.maximum(jnp.dot(values, weight, preferred_element_type=jnp.float32), 0.0).astype(
        jnp.bfloat16
    )


def turned(block, axis, count, shift):
    return lax.ppermute(block, axis, [(i, (i + shift) % count) for i in range(count)])


def coded(indices, lengths):
    slots = lax.broadcasted_iota(jnp.int32, indices.shape, 2)
    return jnp.where(slots < lengths[:, :, None], indices, 32768)


def body(
    dense_input,
    bottom_first,
    bottom_second,
    bottom_third,
    wide_tables,
    narrow_tables,
    wide_indices,
    wide_lengths,
    narrow_indices,
    narrow_lengths,
    wide_projection,
    narrow_projection,
    top_first,
    top_last,
):
    own_table = lax.axis_index(TABLES)
    place = jnp.stack([lax.axis_index("x"), lax.axis_index("row")]).astype(jnp.int32)

    words = coded(wide_indices, wide_lengths) | (coded(narrow_indices, narrow_lengths) << 16)
    words = jnp.transpose(words, (1, 2, 0)).reshape(32, 1, LANES)
    words = jnp.broadcast_to(words, (32, 8, LANES)).reshape(256, LANES)
    words = lax.all_to_all(words, HOME, 0, 0, tiled=True)

    wide_weight = lax.dynamic_index_in_dim(wide_projection, own_table, 0, keepdims=False)
    narrow_weight = lax.dynamic_index_in_dim(narrow_projection, own_table, 0, keepdims=False)
    wide_rows = jnp.dot(wide_tables, wide_weight, preferred_element_type=jnp.float32)
    narrow_rows = jnp.dot(narrow_tables, narrow_weight, preferred_element_type=jnp.float32)

    keep, send = pool(place, words, wide_rows, narrow_rows)
    other = turned(send, "row", 2, 1)
    both = (keep.astype(jnp.float32) + other.astype(jnp.float32)).astype(jnp.bfloat16)
    both = both.reshape(4, 512, 256)
    total = both[0].astype(jnp.float32)
    for shift in (1, 2, 3):
        total = total + turned(both[shift], "x", 4, shift).astype(jnp.float32)
    home = lax.all_to_all(
        total.astype(jnp.bfloat16).reshape(32, BAGS, 256), TABLES, 0, 0, tiled=True
    )

    bottom = dense_layer(
        dense_layer(dense_layer(dense_input, bottom_first), bottom_second), bottom_third
    )
    features = jnp.concatenate([bottom[None], home[:, :, :LANES], home[:, :, LANES:]], 0)
    products = jnp.einsum("fbe,gbe->bfg", features, features, preferred_element_type=jnp.float32)
    pairs = jnp.concatenate([products[:, f, f + 1 :] for f in range(64)], 1)
    joined = jnp.concatenate([bottom.astype(jnp.float32), pairs], 1).astype(jnp.bfloat16)
    hidden = dense_layer(joined, top_first)
    logits = jnp.dot(hidden, top_last, preferred_element_type=jnp.float32)
    return (hidden, logits)


def solution(mesh):
    fine = Mesh(mesh.devices.reshape(4, 8, 4, 2), HOME)
    split = P(HOME)
    in_specs = (split, P(), P(), P()) + (split,) * 6 + (P(),) * 4
    return jax.shard_map(
        body, mesh=fine, in_specs=in_specs, out_specs=(split, split), check_vma=False
    )
```

```python
import jax
import jax.numpy as jnp
from jax import lax
from jax.experimental import pallas as pl
from jax.experimental.pallas import tpu as pltpu
from jax.sharding import Mesh
from jax.sharding import PartitionSpec as P

SLOTS = 8
BAGS = 16
LANES = 128
ROWS = 4096
SOURCES = 256
FEATURES = 65
PITCH = 72
INTER = 2208
VMEM = pl.BlockSpec(memory_space=pltpu.VMEM)


def drawn_left(packed, field, unit, bits):
    for bit in range(bits):
        moved = jnp.where((packed & (1 << (field + bit))) != 0, packed, 0)
        packed = packed - moved + pltpu.roll(moved, LANES - (unit << bit), 1)
    return packed


def counted(flags, before):
    return jnp.dot(
        jnp.where(flags, 1.0, 0.0).astype(jnp.bfloat16), before, preferred_element_type=jnp.float32
    ).astype(jnp.int32)


def as_matrix(flags):
    return jnp.where(flags, 1.0, 0.0).astype(jnp.bfloat16)


def pool_kernel(place_ref, words_ref, wide_ref, narrow_ref, keep_ref, send_ref,
                wide_rows, narrow_rows, wide_sum, narrow_sum, firsts_v, more_v, lists_v,
                firsts, lists, sems):
    tables = [
        pltpu.make_async_copy(wide_ref, wide_rows.at[pl.ds(0, ROWS)], sems.at[0]),
        pltpu.make_async_copy(narrow_ref, narrow_rows.at[pl.ds(0, ROWS)], sems.at[1]),
    ]
    for copy in tables:
        copy.start()
    my_x = place_ref[0]
    my_row = place_ref[1]
    shard = my_x * 2 + my_row
    wide_rows[pl.ds(ROWS, 8), :] = jnp.zeros((8, LANES), jnp.float32)
    narrow_rows[pl.ds(ROWS, 8), :] = jnp.zeros((8, LANES), jnp.float32)
    at = lax.broadcasted_iota(jnp.int32, (LANES, LANES), 0)
    to = lax.broadcasted_iota(jnp.int32, (LANES, LANES), 1)
    same_bag = as_matrix(((at & 15) == (to & 15)) & (at < to))
    any_bag = as_matrix(at < to)

    def base_of(source):
        yz = source >> 3
        x = (source >> 1) & 3
        row = source & 1
        return ((row ^ my_row) << 11) + (((x - my_x) & 3) << 9) + (yz << 4)

    lane = lax.broadcasted_iota(jnp.int32, (SOURCES, LANES), 1)
    target = base_of(lax.broadcasted_iota(jnp.int32, (SOURCES, LANES), 0)) + (lane & 15)
    words = words_ref[...]
    most = jnp.int32(0)
    picks = []
    for kind, value in enumerate((words & 65535, (words >> 16) & 65535)):
        local = (value >> 12) == shard
        gap = (lane >> 4) - counted(local, same_bag)
        packed = jnp.where(local, (value & 4095) | (gap << 12) | (1 << 15), 0)
        packed = drawn_left(packed, 12, BAGS, 3)
        picks.append(jnp.where(packed != 0, packed & 4095, ROWS))
        more = (packed != 0) & (lane >= BAGS)
        before = counted(more, any_bag)
        most = jnp.maximum(most, jnp.max(before + more.astype(jnp.int32)))
        extra = (packed & 4095) | (target << 12) | ((lane - before) << 24) | jnp.int32(-(2**31))
        extra = drawn_left(jnp.where(more, extra, 0), 24, 1, 7)
        more_v[kind] = jnp.transpose(extra)
    pair = jnp.where(lane < BAGS, picks[0] | (picks[1] << 16), 0)
    line = pair[0:32]
    for j in range(1, 8):
        line = line + pltpu.roll(pair[j * 32 : (j + 1) * 32], j * BAGS, 1)
    firsts_v[...] = line
    first_copy = pltpu.make_async_copy(firsts_v, firsts, sems.at[2])
    first_copy.start()
    first_copy.wait()
    for copy in tables:
        copy.wait()

    def one_group(group, _):
        for j in range(8):
            base = pl.multiple_of(base_of(j * 32 + group), BAGS)
            for low in range(0, BAGS, 8):
                bags = range(low, low + 8)
                both = [firsts[group, j * BAGS + bag] for bag in bags]
                wide = [wide_rows[pl.ds(pair & 65535, 1), :] for pair in both]
                narrow = [narrow_rows[pl.ds(pair >> 16, 1), :] for pair in both]
                for bag, row in zip(bags, wide):
                    wide_sum[pl.ds(base + bag, 1), :] = row
                for bag, row in zip(bags, narrow):
                    narrow_sum[pl.ds(base + bag, 1), :] = row
        return 0

    lax.fori_loop(0, 32, one_group, 0)

    lane32 = lax.broadcasted_iota(jnp.int32, (32, LANES), 1)

    def one_block(block, _):
        rows = pl.ds(pl.multiple_of(block * 8, 8), 8)
        held = jnp.concatenate(
            [more_v[kind, rows, half * LANES : (half + 1) * LANES] for kind in (0, 1) for half in (0, 1)], 0
        )
        used = held < 0
        before = counted(used, any_bag)
        total = jnp.sum(used.astype(jnp.int32), axis=1, keepdims=True)
        packed = jnp.where(used, (held & 0xFFFFFF) | ((lane32 - before) << 24), 0)
        packed = drawn_left(packed, 24, 1, 7) & 0xFFFFFF
        lists_v[...] = packed | jnp.where(lane32 == 0, total << 24, 0)
        copy = pltpu.make_async_copy(lists_v, lists, sems.at[3])
        copy.start()
        copy.wait()

        def add(low, rows, sums):
            def one_list(k, _):
                def some(low, count):
                    entries = [lists[k, low + i] for i in range(count)]
                    places = [pl.ds((entry >> 12) & 4095, 1) for entry in entries]
                    values = [
                        sums[place, :] + rows[pl.ds(entry & 4095, 1), :]
                        for entry, place in zip(entries, places)
                    ]
                    for place, value in zip(places, values):
                        sums[place, :] = value

                def four(i, _):
                    some(i * 4, 4)
                    return 0

                def one(i, _):
                    some(i, 1)
                    return 0

                count = lax.shift_right_logical(lists[k, 0], 24)
                lax.fori_loop(0, count // 4, four, 0)
                lax.fori_loop(count // 4 * 4, count, one, 0)
                return 0

            lax.fori_loop(low, low + 16, one_list, 0)

        add(0, wide_rows, wide_sum)
        add(16, narrow_rows, narrow_sum)
        return 0

    lax.fori_loop(0, (most + 7) >> 3, one_block, 0)

    def finish(ref, start):
        def one(i, _):
            rows = pl.ds(pl.multiple_of(i * 128, 128), 128)
            source = pl.ds(pl.multiple_of(start + i * 128, 128), 128)
            ref[rows, 0:LANES] = wide_sum[source, :].astype(jnp.bfloat16)
            ref[rows, LANES:] = narrow_sum[source, :].astype(jnp.bfloat16)
            return 0

        lax.fori_loop(0, 16, one, 0)

    finish(keep_ref, 0)
    finish(send_ref, 2048)


def pool(place, words, wide, narrow):
    vmem = pl.BlockSpec(memory_space=pltpu.VMEM)
    half = jax.ShapeDtypeStruct((2048, 256), jnp.bfloat16)
    return pl.pallas_call(
        pool_kernel,
        out_shape=(half, half),
        in_specs=[pl.BlockSpec(memory_space=pltpu.SMEM), vmem,
                  pl.BlockSpec(memory_space=pl.ANY), pl.BlockSpec(memory_space=pl.ANY)],
        out_specs=(vmem, vmem),
        scratch_shapes=[
            pltpu.VMEM((ROWS + 8, LANES), jnp.float32),
            pltpu.VMEM((ROWS + 8, LANES), jnp.float32),
            pltpu.VMEM((ROWS, LANES), jnp.float32),
            pltpu.VMEM((ROWS, LANES), jnp.float32),
            pltpu.VMEM((32, LANES), jnp.int32),
            pltpu.VMEM((2, LANES, SOURCES), jnp.int32),
            pltpu.VMEM((32, LANES), jnp.int32),
            pltpu.SMEM((32, LANES), jnp.int32),
            pltpu.SMEM((32, LANES), jnp.int32),
            pltpu.SemaphoreType.DMA((4,)),
        ],
        compiler_params=pltpu.CompilerParams(vmem_limit_bytes=60 * 1024 * 1024),
    )(place, words, wide, narrow)


def top_kernel(bottom_ref, home_ref, first_ref, last_ref, hidden_ref, logits_ref, stack, grams, joined):
    bottom = bottom_ref[...].astype(jnp.float32)
    stack[:, 0:1, :] = bottom[:, None, :]
    for table in range(32):
        both = home_ref[table].astype(jnp.float32)
        stack[:, 1 + table : 2 + table, :] = both[:, None, :LANES]
        stack[:, 33 + table : 34 + table, :] = both[:, None, LANES:]
    stack[:, FEATURES:, :] = jnp.zeros((BAGS, PITCH - FEATURES, LANES), jnp.float32)
    for bag in range(BAGS):
        features = stack[bag].astype(jnp.bfloat16)
        grams[bag * PITCH : (bag + 1) * PITCH, 0:PITCH] = lax.dot_general(
            features, features, (((1,), (1,)), ((), ())), preferred_element_type=jnp.float32
        )
    joined[:, 0:LANES] = bottom
    at = LANES
    for f in range(FEATURES - 1):
        count = FEATURES - 1 - f
        line = grams[pl.ds(f, BAGS, stride=PITCH), :]
        joined[:, at : at + count] = line[:, f + 1 : FEATURES]
        at += count
    hidden = jnp.dot(
        joined[...].astype(jnp.bfloat16), first_ref[...], preferred_element_type=jnp.float32
    )
    hidden = jnp.maximum(hidden, 0.0).astype(jnp.bfloat16)
    hidden_ref[...] = hidden
    logits_ref[...] = jnp.sum(
        hidden.astype(jnp.float32) * last_ref[...].astype(jnp.float32), axis=1, keepdims=True
    )


def top(bottom, home, top_first, top_last):
    return pl.pallas_call(
        top_kernel,
        out_shape=(
            jax.ShapeDtypeStruct((BAGS, 1024), jnp.bfloat16),
            jax.ShapeDtypeStruct((BAGS, 1), jnp.float32),
        ),
        in_specs=[VMEM] * 4,
        out_specs=(VMEM, VMEM),
        scratch_shapes=[
            pltpu.VMEM((BAGS, PITCH, LANES), jnp.float32),
            pltpu.VMEM((BAGS * PITCH, LANES), jnp.float32),
            pltpu.VMEM((BAGS, INTER), jnp.float32),
        ],
        compiler_params=pltpu.CompilerParams(vmem_limit_bytes=16 * 1024 * 1024),
        name="top",
    )(bottom, home, top_first, top_last.reshape(1, 1024))


HOME = ("y", "z", "x", "row")
TABLES = ("y", "z")


def dense_layer(values, weight):
    return jnp.maximum(jnp.dot(values, weight, preferred_element_type=jnp.float32), 0.0).astype(
        jnp.bfloat16
    )


def turned(block, axis, count, shift):
    return lax.ppermute(block, axis, [(i, (i + shift) % count) for i in range(count)])


def coded(indices, lengths):
    slots = lax.broadcasted_iota(jnp.int32, indices.shape, 2)
    return jnp.where(slots < lengths[:, :, None], indices, 32768)


def body(
    dense_input,
    bottom_first,
    bottom_second,
    bottom_third,
    wide_tables,
    narrow_tables,
    wide_indices,
    wide_lengths,
    narrow_indices,
    narrow_lengths,
    wide_projection,
    narrow_projection,
    top_first,
    top_last,
):
    own_table = lax.axis_index(TABLES)
    place = jnp.stack([lax.axis_index("x"), lax.axis_index("row")]).astype(jnp.int32)

    words = coded(wide_indices, wide_lengths) | (coded(narrow_indices, narrow_lengths) << 16)
    words = jnp.transpose(words, (1, 2, 0)).reshape(32, 1, LANES)
    words = jnp.broadcast_to(words, (32, 8, LANES)).reshape(256, LANES)
    words = lax.all_to_all(words, HOME, 0, 0, tiled=True)

    wide_weight = lax.dynamic_index_in_dim(wide_projection, own_table, 0, keepdims=False)
    narrow_weight = lax.dynamic_index_in_dim(narrow_projection, own_table, 0, keepdims=False)
    wide_rows = jnp.dot(wide_tables, wide_weight, preferred_element_type=jnp.float32)
    narrow_rows = jnp.dot(narrow_tables, narrow_weight, preferred_element_type=jnp.float32)

    keep, send = pool(place, words, wide_rows, narrow_rows)
    other = turned(send, "row", 2, 1)
    both = (keep.astype(jnp.float32) + other.astype(jnp.float32)).astype(jnp.bfloat16)
    both = both.reshape(4, 512, 256)
    total = both[0].astype(jnp.float32)
    for shift in (1, 2, 3):
        total = total + turned(both[shift], "x", 4, shift).astype(jnp.float32)
    home = lax.all_to_all(
        total.astype(jnp.bfloat16).reshape(32, BAGS, 256), TABLES, 0, 0, tiled=True
    )

    bottom = dense_layer(
        dense_layer(dense_layer(dense_input, bottom_first), bottom_second), bottom_third
    )
    hidden, logits = top(bottom, home, top_first, top_last)
    return (hidden, logits.reshape(BAGS))


def solution(mesh):
    fine = Mesh(mesh.devices.reshape(4, 8, 4, 2), HOME)
    split = P(HOME)
    in_specs = (split, P(), P(), P()) + (split,) * 6 + (P(),) * 4
    return jax.shard_map(
        body, mesh=fine, in_specs=in_specs, out_specs=(split, split), check_vma=False
    )
```

```python
import jax
import jax.numpy as jnp
from jax import lax
from jax.experimental import pallas as pl
from jax.experimental.pallas import tpu as pltpu
from jax.sharding import Mesh
from jax.sharding import PartitionSpec as P

BAGS = 16
LANES = 128
ROWS = 4096
SOURCES = 256
LINES = 32
BLOCKS = 16
SHIFTS = (1, 3, 2, 0)
FEATURES = 65
PITCH = 72
INTER = 2208
TOP = 1024
LIMIT = pltpu.CompilerParams(vmem_limit_bytes=60 * 1024 * 1024)
VMEM = pl.BlockSpec(memory_space=pltpu.VMEM)
SMEM = pl.BlockSpec(memory_space=pltpu.SMEM)
ANY = pl.BlockSpec(memory_space=pl.ANY)


def drawn_left(packed, field, unit, bits):
    for bit in range(bits):
        moved = jnp.where((packed & (1 << (field + bit))) != 0, packed, 0)
        packed = packed - moved + pltpu.roll(moved, LANES - (unit << bit), 1)
    return packed


def as_matrix(flags):
    return jnp.where(flags, 1.0, 0.0).astype(jnp.bfloat16)


def counted(flags, before):
    return jnp.dot(as_matrix(flags), before, preferred_element_type=jnp.float32).astype(jnp.int32)


def prepared(place_ref, words_ref, firsts_ref, more_v, lists_ref):
    my_x = place_ref[0]
    my_row = place_ref[1]
    shard = my_x * 2 + my_row
    at = lax.broadcasted_iota(jnp.int32, (LANES, LANES), 0)
    to = lax.broadcasted_iota(jnp.int32, (LANES, LANES), 1)
    same_bag = as_matrix(((at & 15) == (to & 15)) & (at < to))
    any_bag = as_matrix(at < to)
    lane = lax.broadcasted_iota(jnp.int32, (SOURCES, LANES), 1)
    target = lax.broadcasted_iota(jnp.int32, (SOURCES, LANES), 0) * BAGS + (lane & 15)
    parts = []
    for shift in SHIFTS:
        for row in (0, 1):
            start = ((my_x + shift) & 3) * 2 + (my_row ^ row)
            parts.append(words_ref[pl.ds(start, 32, stride=8), :])
    words = jnp.concatenate(parts, 0)
    most = jnp.int32(0)
    picks = []
    for kind, value in enumerate((words & 65535, (words >> 16) & 65535)):
        local = (value >> 12) == shard
        gap = (lane >> 4) - counted(local, same_bag)
        packed = jnp.where(local, (value & 4095) | (gap << 12) | (1 << 15), 0)
        packed = drawn_left(packed, 12, BAGS, 3)
        picks.append(jnp.where(packed != 0, packed & 4095, ROWS))
        more = (packed != 0) & (lane >= BAGS)
        before = counted(more, any_bag)
        most = jnp.maximum(most, jnp.max(before + more.astype(jnp.int32)))
        extra = (packed & 4095) | (target << 12) | ((lane - before) << 24) | jnp.int32(-(2**31))
        extra = drawn_left(jnp.where(more, extra, 0), 24, 1, 7)
        more_v[kind] = jnp.transpose(extra)
    pair = jnp.where(lane < BAGS, picks[0] | (picks[1] << 16), 0)
    for part in range(4):
        line = pair[part * 64 : part * 64 + 8]
        for j in range(1, 8):
            low = part * 64 + j * 8
            line = line + pltpu.roll(pair[low : low + 8], j * BAGS, 1)
        firsts_ref[part * 8 : (part + 1) * 8] = line
    lane = lax.broadcasted_iota(jnp.int32, (LINES, LANES), 1)

    def one_block(block, _):
        rows = pl.ds(pl.multiple_of(block * 8, 8), 8)
        held = jnp.concatenate(
            [
                more_v[kind, rows, half * LANES : (half + 1) * LANES]
                for kind in (0, 1)
                for half in (0, 1)
            ],
            0,
        )
        used = held < 0
        before = counted(used, any_bag)
        ones = used.astype(jnp.int32)
        total = jnp.sum(ones, axis=1, keepdims=True)
        part = jnp.sum(jnp.where(lane < 64, ones, 0), axis=1, keepdims=True)
        packed = jnp.where(used, (held & 0xFFFFFF) | ((lane - before) << 24), 0)
        packed = drawn_left(packed, 24, 1, 7) & 0xFFFFFF
        counts = jnp.where(lane == 0, total, 0) + jnp.where(lane == 1, part, 0)
        lists_ref[pl.ds(pl.multiple_of(block * LINES, LINES), LINES), :] = packed | (counts << 24)
        return 0

    blocks = jnp.maximum((most + 7) >> 3, 1)
    lax.fori_loop(0, blocks, one_block, 0)
    return blocks


def pooled(first_part, parts, blocks, first_line, firsts, lists_ref, lists, wide_rows, narrow_rows,
           wide_sum, narrow_sum, keep_ref, send_ref, sem):
    low_row = first_part * 1024
    spans = ((0, 0), (1, 1)) if parts == 3 else ((1, 2),)

    def block_copy(block):
        rows = pl.ds(pl.multiple_of(block * LINES, LINES), LINES)
        return pltpu.make_async_copy(lists_ref.at[rows], lists, sem)

    block_copy(0).start()

    def one_group(group, _):
        for part in range(parts):
            for j in range(8):
                base = pl.multiple_of(part * 1024 + j * 128 + group * BAGS, BAGS)
                for low in range(0, BAGS, 8):
                    bags = range(low, low + 8)
                    both = [firsts[first_line + part * 8 + group, j * BAGS + bag] for bag in bags]
                    wide = [wide_rows[pl.ds(pair & 65535, 1), :] for pair in both]
                    narrow = [narrow_rows[pl.ds(pair >> 16, 1), :] for pair in both]
                    for bag, row in zip(bags, wide):
                        wide_sum[pl.ds(base + bag, 1), :] = row
                    for bag, row in zip(bags, narrow):
                        narrow_sum[pl.ds(base + bag, 1), :] = row
        return 0

    lax.fori_loop(0, 8, one_group, 0)

    def one_block(block, _):
        @pl.when(block > 0)
        def _():
            block_copy(block).start()

        block_copy(block).wait()

        for kind, rows, sums in ((0, wide_rows, wide_sum), (1, narrow_rows, narrow_sum)):

            def some(k, low, count):
                entries = [lists[k, low + i] for i in range(count)]
                places = [pl.ds(((entry >> 12) & 4095) - low_row, 1) for entry in entries]
                values = [
                    sums[place, :] + rows[pl.ds(entry & 4095, 1), :]
                    for entry, place in zip(entries, places)
                ]
                for place, value in zip(places, values):
                    sums[place, :] = value

            for half, span in spans:

                def one_list(k, _, span=span):
                    low, high = 0, lax.shift_right_logical(lists[k, 0], 24)
                    if span:
                        middle = lax.shift_right_logical(lists[k, 1], 24)
                        low, high = (low, middle) if span == 1 else (middle, high)

                    def four(i, _):
                        some(k, low + i * 4, 4)
                        return 0

                    def one(i, _):
                        some(k, i, 1)
                        return 0

                    fours = (high - low) >> 2
                    lax.fori_loop(0, fours, four, 0)
                    lax.fori_loop(low + fours * 4, high, one, 0)
                    return 0

                start = kind * 16 + half * 8
                lax.fori_loop(start, start + 8, one_list, 0)
        return 0

    lax.fori_loop(0, blocks, one_block, 0)

    for part in range(parts):
        for row, ref in enumerate((keep_ref, send_ref)):

            def one(i, _):
                to = pl.ds(pl.multiple_of(part * 512 + i * 128, 128), 128)
                source = pl.ds(pl.multiple_of(part * 1024 + row * 512 + i * 128, 128), 128)
                ref[to, 0:LANES] = wide_sum[source, :].astype(jnp.bfloat16)
                ref[to, LANES:] = narrow_sum[source, :].astype(jnp.bfloat16)
                return 0

            lax.fori_loop(0, 4, one, 0)


def table_copies(wide_ref, narrow_ref, wide_rows, narrow_rows, sems):
    pairs = ((wide_ref, wide_rows), (narrow_ref, narrow_rows))
    copies = []
    for at, (ref, rows) in enumerate(pairs):
        copies.append(pltpu.make_async_copy(ref, rows.at[pl.ds(0, ROWS)], sems.at[at]))
        copies[-1].start()
        rows[pl.ds(ROWS, 8), :] = jnp.zeros((8, LANES), jnp.float32)
    return copies


def first_kernel(place_ref, words_ref, wide_ref, narrow_ref, keep_ref, send_ref, firsts_ref,
                 lists_ref, blocks_ref, more_v, wide_rows, narrow_rows, wide_sum, narrow_sum,
                 firsts, lists, sems):
    copies = table_copies(wide_ref, narrow_ref, wide_rows, narrow_rows, sems)
    blocks = prepared(place_ref, words_ref, firsts_ref, more_v, lists_ref)
    blocks_ref[0] = blocks
    copies.append(pltpu.make_async_copy(firsts_ref, firsts, sems.at[2]))
    copies[-1].start()
    for copy in copies:
        copy.wait()
    pooled(0, 3, blocks, 0, firsts, lists_ref, lists, wide_rows, narrow_rows, wide_sum, narrow_sum,
           keep_ref, send_ref, sems.at[3])


def last_kernel(blocks_ref, firsts_ref, lists_ref, wide_ref, narrow_ref, keep_ref, send_ref,
                wide_rows, narrow_rows, wide_sum, narrow_sum, lists, sems):
    copies = table_copies(wide_ref, narrow_ref, wide_rows, narrow_rows, sems)
    for copy in copies:
        copy.wait()
    pooled(3, 1, blocks_ref[0], 24, firsts_ref, lists_ref, lists, wide_rows, narrow_rows, wide_sum,
           narrow_sum, keep_ref, send_ref, sems.at[2])


def shapes(parts):
    half = jax.ShapeDtypeStruct((parts * 512, 2 * LANES), jnp.bfloat16)
    rows = pltpu.VMEM((ROWS + 8, LANES), jnp.float32)
    sums = pltpu.VMEM((parts * 1024, LANES), jnp.float32)
    cost = pl.CostEstimate(flops=10**6, bytes_accessed=10**7, transcendentals=0)
    return half, [rows, rows, sums, sums], cost


def pool_first(place, words, wide, narrow):
    half, buffers, cost = shapes(3)
    return pl.pallas_call(
        first_kernel,
        out_shape=(
            half,
            half,
            jax.ShapeDtypeStruct((32, LANES), jnp.int32),
            jax.ShapeDtypeStruct((BLOCKS * LINES, LANES), jnp.int32),
            jax.ShapeDtypeStruct((1,), jnp.int32),
        ),
        in_specs=[SMEM, VMEM, ANY, ANY],
        out_specs=(VMEM, VMEM, VMEM, VMEM, SMEM),
        scratch_shapes=[pltpu.VMEM((2, LANES, SOURCES), jnp.int32)]
        + buffers
        + [
            pltpu.SMEM((LINES, LANES), jnp.int32),
            pltpu.SMEM((LINES, LANES), jnp.int32),
            pltpu.SemaphoreType.DMA((4,)),
        ],
        compiler_params=LIMIT,
        cost_estimate=cost,
        name="pool_first",
    )(place, words, wide, narrow)


def pool_last(blocks, firsts, lists, wide, narrow):
    half, buffers, cost = shapes(1)
    return pl.pallas_call(
        last_kernel,
        out_shape=(half, half),
        in_specs=[SMEM, SMEM, ANY, ANY, ANY],
        out_specs=(VMEM, VMEM),
        scratch_shapes=buffers
        + [pltpu.SMEM((LINES, LANES), jnp.int32), pltpu.SemaphoreType.DMA((3,))],
        compiler_params=LIMIT,
        cost_estimate=cost,
        name="pool_last",
    )(blocks, firsts, lists, wide, narrow)


def top_kernel(bottom_ref, home_ref, first_ref, last_ref, hidden_ref, logits_ref, stack, grams, joined):
    bottom = bottom_ref[...].astype(jnp.float32)
    stack[:, 0:1, :] = bottom[:, None, :]
    for table in range(32):
        both = home_ref[table].astype(jnp.float32)
        stack[:, 1 + table : 2 + table, :] = both[:, None, :LANES]
        stack[:, 33 + table : 34 + table, :] = both[:, None, LANES:]
    stack[:, FEATURES:, :] = jnp.zeros((BAGS, PITCH - FEATURES, LANES), jnp.float32)
    for bag in range(BAGS):
        features = stack[bag].astype(jnp.bfloat16)
        grams[bag * PITCH : (bag + 1) * PITCH, 0:PITCH] = lax.dot_general(
            features, features, (((1,), (1,)), ((), ())), preferred_element_type=jnp.float32
        )
    joined[:, 0:LANES] = bottom
    at = LANES
    for f in range(FEATURES - 1):
        count = FEATURES - 1 - f
        line = grams[pl.ds(f, BAGS, stride=PITCH), :]
        joined[:, at : at + count] = line[:, f + 1 : FEATURES]
        at += count
    hidden = jnp.dot(
        joined[...].astype(jnp.bfloat16), first_ref[...], preferred_element_type=jnp.float32
    )
    hidden = jnp.maximum(hidden, 0.0).astype(jnp.bfloat16)
    hidden_ref[...] = hidden
    logits_ref[...] = lax.dot_general(
        last_ref[...], hidden, (((1,), (1,)), ((), ())), preferred_element_type=jnp.float32
    )


def top(bottom, home, top_first, top_last):
    return pl.pallas_call(
        top_kernel,
        out_shape=(
            jax.ShapeDtypeStruct((BAGS, TOP), jnp.bfloat16),
            jax.ShapeDtypeStruct((1, BAGS), jnp.float32),
        ),
        in_specs=[VMEM] * 4,
        out_specs=(VMEM, VMEM),
        scratch_shapes=[
            pltpu.VMEM((BAGS, PITCH, LANES), jnp.float32),
            pltpu.VMEM((BAGS * PITCH, LANES), jnp.float32),
            pltpu.VMEM((BAGS, INTER), jnp.float32),
        ],
        compiler_params=pltpu.CompilerParams(vmem_limit_bytes=16 * 1024 * 1024),
        name="top",
    )(bottom, home, top_first, top_last.reshape(1, TOP))


HOME = ("y", "z", "x", "row")
TABLES = ("y", "z")


def dense_layer(values, weight):
    return jnp.maximum(jnp.dot(values, weight, preferred_element_type=jnp.float32), 0.0).astype(
        jnp.bfloat16
    )


def turned(block, axis, count, shift):
    return lax.ppermute(block, axis, [(i, (i + shift) % count) for i in range(count)])


def added(one, other):
    return (one.astype(jnp.float32) + other.astype(jnp.float32)).astype(jnp.bfloat16)


def coded(indices, lengths):
    slots = lax.broadcasted_iota(jnp.int32, indices.shape, 2)
    return jnp.where(slots < lengths[:, :, None], indices, 32768)


def body(
    dense_input,
    bottom_first,
    bottom_second,
    bottom_third,
    wide_tables,
    narrow_tables,
    wide_indices,
    wide_lengths,
    narrow_indices,
    narrow_lengths,
    wide_projection,
    narrow_projection,
    top_first,
    top_last,
):
    own_table = lax.axis_index(TABLES)
    place = jnp.stack([lax.axis_index("x"), lax.axis_index("row")]).astype(jnp.int32)

    words = coded(wide_indices, wide_lengths) | (coded(narrow_indices, narrow_lengths) << 16)
    words = jnp.transpose(words, (1, 2, 0)).reshape(32, 1, LANES)
    words = jnp.broadcast_to(words, (32, 8, LANES)).reshape(256, LANES)
    words = lax.all_to_all(words, HOME, 0, 0, tiled=True)

    wide_weight = lax.dynamic_index_in_dim(wide_projection, own_table, 0, keepdims=False)
    narrow_weight = lax.dynamic_index_in_dim(narrow_projection, own_table, 0, keepdims=False)
    wide_rows = jnp.dot(wide_tables, wide_weight, preferred_element_type=jnp.float32)
    narrow_rows = jnp.dot(narrow_tables, narrow_weight, preferred_element_type=jnp.float32)

    keep, send, firsts, lists, blocks = pool_first(place, words, wide_rows, narrow_rows)
    both = added(keep, turned(send, "row", 2, 1))
    both, lists = lax.optimization_barrier((both, lists))
    moved = [
        turned(both[at * 512 : (at + 1) * 512], "x", 4, shift)
        for at, shift in enumerate(SHIFTS[:3])
    ]
    keep, send = pool_last(blocks, firsts, lists, wide_rows, narrow_rows)
    total = keep.astype(jnp.float32)
    for part in moved + [turned(send, "row", 2, 1)]:
        total = total + part.astype(jnp.float32)
    home = lax.all_to_all(
        total.astype(jnp.bfloat16).reshape(32, BAGS, 256), TABLES, 0, 0, tiled=True
    )

    bottom = dense_layer(
        dense_layer(dense_layer(dense_input, bottom_first), bottom_second), bottom_third
    )
    hidden, logits = top(bottom, home, top_first, top_last)
    return (hidden, logits.reshape(BAGS))


def solution(mesh):
    fine = Mesh(mesh.devices.reshape(4, 8, 4, 2), HOME)
    split = P(HOME)
    in_specs = (split, P(), P(), P()) + (split,) * 6 + (P(),) * 4
    return jax.shard_map(
        body, mesh=fine, in_specs=in_specs, out_specs=(split, split), check_vma=False
    )
```

```python
import jax
import jax.numpy as jnp
from jax import lax
from jax.experimental import pallas as pl
from jax.experimental.pallas import tpu as pltpu
from jax.sharding import Mesh
from jax.sharding import PartitionSpec as P

BAGS = 16
LANES = 128
ROWS = 4096
SOURCES = 256
LINES = 32
BLOCKS = 16
SHIFTS = (1, 3, 2, 0)
FEATURES = 65
PITCH = 72
INTER = 2208
TOP = 1024
LIMIT = pltpu.CompilerParams(vmem_limit_bytes=24 * 1024 * 1024)
VMEM = pl.BlockSpec(memory_space=pltpu.VMEM)
SMEM = pl.BlockSpec(memory_space=pltpu.SMEM)
ANY = pl.BlockSpec(memory_space=pl.ANY)
HBM = pl.BlockSpec(memory_space=pltpu.HBM)


def drawn_left(packed, field, unit, bits):
    for bit in range(bits):
        moved = jnp.where((packed & (1 << (field + bit))) != 0, packed, 0)
        packed = packed - moved + pltpu.roll(moved, LANES - (unit << bit), 1)
    return packed


def as_matrix(flags):
    return jnp.where(flags, 1.0, 0.0).astype(jnp.bfloat16)


def counted(flags, before):
    return jnp.dot(as_matrix(flags), before, preferred_element_type=jnp.float32).astype(jnp.int32)


def prepared(place_ref, words_ref, firsts_ref, more_v, lists_ref):
    my_x = place_ref[0]
    my_row = place_ref[1]
    shard = my_x * 2 + my_row
    at = lax.broadcasted_iota(jnp.int32, (LANES, LANES), 0)
    to = lax.broadcasted_iota(jnp.int32, (LANES, LANES), 1)
    same_bag = as_matrix(((at & 15) == (to & 15)) & (at < to))
    any_bag = as_matrix(at < to)
    lane = lax.broadcasted_iota(jnp.int32, (SOURCES, LANES), 1)
    target = lax.broadcasted_iota(jnp.int32, (SOURCES, LANES), 0) * BAGS + (lane & 15)
    parts = []
    for shift in SHIFTS:
        for row in (0, 1):
            start = ((my_x + shift) & 3) * 2 + (my_row ^ row)
            parts.append(words_ref[pl.ds(start, 32, stride=8), :])
    words = jnp.concatenate(parts, 0)
    most = jnp.int32(0)
    picks = []
    for kind, value in enumerate((words & 65535, (words >> 16) & 65535)):
        local = (value >> 12) == shard
        gap = (lane >> 4) - counted(local, same_bag)
        packed = jnp.where(local, (value & 4095) | (gap << 12) | (1 << 15), 0)
        packed = drawn_left(packed, 12, BAGS, 3)
        picks.append(jnp.where(packed != 0, packed & 4095, ROWS))
        more = (packed != 0) & (lane >= BAGS)
        before = counted(more, any_bag)
        most = jnp.maximum(most, jnp.max(before + more.astype(jnp.int32)))
        extra = (packed & 4095) | (target << 12) | ((lane - before) << 24) | jnp.int32(-(2**31))
        extra = drawn_left(jnp.where(more, extra, 0), 24, 1, 7)
        more_v[kind] = jnp.transpose(extra)
    pair = jnp.where(lane < BAGS, picks[0] | (picks[1] << 16), 0)
    for part in range(4):
        line = pair[part * 64 : part * 64 + 8]
        for j in range(1, 8):
            low = part * 64 + j * 8
            line = line + pltpu.roll(pair[low : low + 8], j * BAGS, 1)
        firsts_ref[part * 8 : (part + 1) * 8] = line
    lane = lax.broadcasted_iota(jnp.int32, (LINES, LANES), 1)

    def one_block(block, _):
        rows = pl.ds(pl.multiple_of(block * 8, 8), 8)
        held = jnp.concatenate(
            [
                more_v[kind, rows, half * LANES : (half + 1) * LANES]
                for kind in (0, 1)
                for half in (0, 1)
            ],
            0,
        )
        used = held < 0
        before = counted(used, any_bag)
        ones = used.astype(jnp.int32)
        total = jnp.sum(ones, axis=1, keepdims=True)
        part = jnp.sum(jnp.where(lane < 64, ones, 0), axis=1, keepdims=True)
        packed = jnp.where(used, (held & 0xFFFFFF) | ((lane - before) << 24), 0)
        packed = drawn_left(packed, 24, 1, 7) & 0xFFFFFF
        counts = jnp.where(lane == 0, total, 0) + jnp.where(lane == 1, part, 0)
        lists_ref[pl.ds(pl.multiple_of(block * LINES, LINES), LINES), :] = packed | (counts << 24)
        return 0

    blocks = jnp.maximum((most + 7) >> 3, 1)
    lax.fori_loop(0, blocks, one_block, 0)
    return blocks


def pooled(first_part, parts, blocks, first_line, firsts, lists_ref, lists, wide_rows, narrow_rows,
           wide_sum, narrow_sum, keep_ref, send_ref, sem):
    low_row = first_part * 1024
    spans = ((0, 0), (1, 1)) if parts == 3 else ((1, 2),)

    def block_copy(block):
        rows = pl.ds(pl.multiple_of(block * LINES, LINES), LINES)
        return pltpu.make_async_copy(lists_ref.at[rows], lists, sem)

    block_copy(0).start()

    def one_group(group, _):
        for part in range(parts):
            for j in range(8):
                base = pl.multiple_of(part * 1024 + j * 128 + group * BAGS, BAGS)
                for low in range(0, BAGS, 8):
                    bags = range(low, low + 8)
                    both = [firsts[first_line + part * 8 + group, j * BAGS + bag] for bag in bags]
                    wide = [wide_rows[pl.ds(pair & 65535, 1), :] for pair in both]
                    narrow = [narrow_rows[pl.ds(pair >> 16, 1), :] for pair in both]
                    for bag, row in zip(bags, wide):
                        wide_sum[pl.ds(base + bag, 1), :] = row
                    for bag, row in zip(bags, narrow):
                        narrow_sum[pl.ds(base + bag, 1), :] = row
        return 0

    lax.fori_loop(0, 8, one_group, 0)

    def one_block(block, _):
        @pl.when(block > 0)
        def _():
            block_copy(block).start()

        block_copy(block).wait()

        for kind, rows, sums in ((0, wide_rows, wide_sum), (1, narrow_rows, narrow_sum)):

            def some(k, low, count):
                entries = [lists[k, low + i] for i in range(count)]
                places = [pl.ds(((entry >> 12) & 4095) - low_row, 1) for entry in entries]
                values = [
                    sums[place, :] + rows[pl.ds(entry & 4095, 1), :]
                    for entry, place in zip(entries, places)
                ]
                for place, value in zip(places, values):
                    sums[place, :] = value

            for half, span in spans:

                def one_list(k, _, span=span):
                    low, high = 0, lax.shift_right_logical(lists[k, 0], 24)
                    if span:
                        middle = lax.shift_right_logical(lists[k, 1], 24)
                        low, high = (low, middle) if span == 1 else (middle, high)

                    def four(i, _):
                        some(k, low + i * 4, 4)
                        return 0

                    def one(i, _):
                        some(k, i, 1)
                        return 0

                    fours = (high - low) >> 2
                    lax.fori_loop(0, fours, four, 0)
                    lax.fori_loop(low + fours * 4, high, one, 0)
                    return 0

                start = kind * 16 + half * 8
                lax.fori_loop(start, start + 8, one_list, 0)
        return 0

    lax.fori_loop(0, blocks, one_block, 0)

    for part in range(parts):
        for row, ref in enumerate((keep_ref, send_ref)):

            def one(i, _):
                to = pl.ds(pl.multiple_of(part * 512 + i * 128, 128), 128)
                source = pl.ds(pl.multiple_of(part * 1024 + row * 512 + i * 128, 128), 128)
                ref[to, 0:LANES] = wide_sum[source, :].astype(jnp.bfloat16)
                ref[to, LANES:] = narrow_sum[source, :].astype(jnp.bfloat16)
                return 0

            lax.fori_loop(0, 4, one, 0)


def table_copies(wide_ref, narrow_ref, wide_rows, narrow_rows, sems):
    pairs = ((wide_ref, wide_rows), (narrow_ref, narrow_rows))
    copies = []
    for at, (ref, rows) in enumerate(pairs):
        copies.append(pltpu.make_async_copy(ref, rows.at[pl.ds(0, ROWS)], sems.at[at]))
        copies[-1].start()
        rows[pl.ds(ROWS, 8), :] = jnp.zeros((8, LANES), jnp.float32)
    return copies


def first_kernel(place_ref, words_ref, wide_ref, narrow_ref, keep_ref, send_ref, firsts_ref,
                 lists_ref, blocks_ref, more_v, wide_rows, narrow_rows, wide_sum, narrow_sum,
                 firsts, lists, sems):
    copies = table_copies(wide_ref, narrow_ref, wide_rows, narrow_rows, sems)
    blocks = prepared(place_ref, words_ref, firsts_ref, more_v, lists_ref)
    blocks_ref[0] = blocks
    copies.append(pltpu.make_async_copy(firsts_ref, firsts, sems.at[2]))
    copies[-1].start()
    for copy in copies:
        copy.wait()
    pooled(0, 3, blocks, 0, firsts, lists_ref, lists, wide_rows, narrow_rows, wide_sum, narrow_sum,
           keep_ref, send_ref, sems.at[3])


def last_kernel(blocks_ref, firsts_ref, lists_ref, wide_ref, narrow_ref, keep_ref, send_ref,
                wide_rows, narrow_rows, wide_sum, narrow_sum, lists, sems):
    copies = table_copies(wide_ref, narrow_ref, wide_rows, narrow_rows, sems)
    for copy in copies:
        copy.wait()
    pooled(3, 1, blocks_ref[0], 24, firsts_ref, lists_ref, lists, wide_rows, narrow_rows, wide_sum,
           narrow_sum, keep_ref, send_ref, sems.at[2])


def shapes(parts):
    half = jax.ShapeDtypeStruct((parts * 512, 2 * LANES), jnp.bfloat16)
    rows = pltpu.VMEM((ROWS + 8, LANES), jnp.float32)
    sums = pltpu.VMEM((parts * 1024, LANES), jnp.float32)
    cost = pl.CostEstimate(flops=10**6, bytes_accessed=10**7, transcendentals=0)
    return half, [rows, rows, sums, sums], cost


def pool_first(place, words, wide, narrow):
    half, buffers, cost = shapes(3)
    return pl.pallas_call(
        first_kernel,
        out_shape=(
            half,
            half,
            jax.ShapeDtypeStruct((32, LANES), jnp.int32),
            jax.ShapeDtypeStruct((BLOCKS * LINES, LANES), jnp.int32),
            jax.ShapeDtypeStruct((1,), jnp.int32),
        ),
        in_specs=[SMEM, VMEM, HBM, HBM],
        out_specs=(VMEM, VMEM, VMEM, VMEM, SMEM),
        scratch_shapes=[pltpu.VMEM((2, LANES, SOURCES), jnp.int32)]
        + buffers
        + [
            pltpu.SMEM((LINES, LANES), jnp.int32),
            pltpu.SMEM((LINES, LANES), jnp.int32),
            pltpu.SemaphoreType.DMA((4,)),
        ],
        compiler_params=LIMIT,
        cost_estimate=cost,
        name="pool_first",
    )(place, words, wide, narrow)


def pool_last(blocks, firsts, lists, wide, narrow):
    half, buffers, cost = shapes(1)
    return pl.pallas_call(
        last_kernel,
        out_shape=(half, half),
        in_specs=[SMEM, SMEM, ANY, HBM, HBM],
        out_specs=(VMEM, VMEM),
        scratch_shapes=buffers
        + [pltpu.SMEM((LINES, LANES), jnp.int32), pltpu.SemaphoreType.DMA((3,))],
        compiler_params=LIMIT,
        cost_estimate=cost,
        name="pool_last",
    )(blocks, firsts, lists, wide, narrow)


def top_kernel(bottom_ref, home_ref, first_ref, last_ref, hidden_ref, logits_ref, stack, grams, joined):
    bottom = bottom_ref[...].astype(jnp.float32)
    stack[:, 0:1, :] = bottom[:, None, :]
    for table in range(32):
        both = home_ref[table].astype(jnp.float32)
        stack[:, 1 + table : 2 + table, :] = both[:, None, :LANES]
        stack[:, 33 + table : 34 + table, :] = both[:, None, LANES:]
    stack[:, FEATURES:, :] = jnp.zeros((BAGS, PITCH - FEATURES, LANES), jnp.float32)
    for bag in range(BAGS):
        features = stack[bag].astype(jnp.bfloat16)
        grams[bag * PITCH : (bag + 1) * PITCH, 0:PITCH] = lax.dot_general(
            features, features, (((1,), (1,)), ((), ())), preferred_element_type=jnp.float32
        )
    joined[:, 0:LANES] = bottom
    at = LANES
    for f in range(FEATURES - 1):
        count = FEATURES - 1 - f
        line = grams[pl.ds(f, BAGS, stride=PITCH), :]
        joined[:, at : at + count] = line[:, f + 1 : FEATURES]
        at += count
    hidden = jnp.dot(
        joined[...].astype(jnp.bfloat16), first_ref[...], preferred_element_type=jnp.float32
    )
    hidden = jnp.maximum(hidden, 0.0).astype(jnp.bfloat16)
    hidden_ref[...] = hidden
    logits_ref[...] = lax.dot_general(
        last_ref[...], hidden, (((1,), (1,)), ((), ())), preferred_element_type=jnp.float32
    )


def top(bottom, home, top_first, top_last):
    return pl.pallas_call(
        top_kernel,
        out_shape=(
            jax.ShapeDtypeStruct((BAGS, TOP), jnp.bfloat16),
            jax.ShapeDtypeStruct((1, BAGS), jnp.float32),
        ),
        in_specs=[VMEM] * 4,
        out_specs=(VMEM, VMEM),
        scratch_shapes=[
            pltpu.VMEM((BAGS, PITCH, LANES), jnp.float32),
            pltpu.VMEM((BAGS * PITCH, LANES), jnp.float32),
            pltpu.VMEM((BAGS, INTER), jnp.float32),
        ],
        compiler_params=pltpu.CompilerParams(vmem_limit_bytes=16 * 1024 * 1024),
        name="top",
    )(bottom, home, top_first, top_last.reshape(1, TOP))


HOME = ("y", "z", "x", "row")
TABLES = ("y", "z")


def dense_layer(values, weight):
    return jnp.maximum(jnp.dot(values, weight, preferred_element_type=jnp.float32), 0.0).astype(
        jnp.bfloat16
    )


def turned(block, axis, count, shift):
    return lax.ppermute(block, axis, [(i, (i + shift) % count) for i in range(count)])


def added(one, other):
    return (one.astype(jnp.float32) + other.astype(jnp.float32)).astype(jnp.bfloat16)


def coded(indices, lengths):
    slots = lax.broadcasted_iota(jnp.int32, indices.shape, 2)
    return jnp.where(slots < lengths[:, :, None], indices, 32768)


def body(
    dense_input,
    bottom_first,
    bottom_second,
    bottom_third,
    wide_tables,
    narrow_tables,
    wide_indices,
    wide_lengths,
    narrow_indices,
    narrow_lengths,
    wide_projection,
    narrow_projection,
    top_first,
    top_last,
):
    own_table = lax.axis_index(TABLES)
    place = jnp.stack([lax.axis_index("x"), lax.axis_index("row")]).astype(jnp.int32)

    words = coded(wide_indices, wide_lengths) | (coded(narrow_indices, narrow_lengths) << 16)
    words = jnp.transpose(words, (1, 2, 0)).reshape(32, 1, LANES)
    words = jnp.broadcast_to(words, (32, 8, LANES)).reshape(256, LANES)
    words = lax.all_to_all(words, HOME, 0, 0, tiled=True)

    wide_weight = lax.dynamic_index_in_dim(wide_projection, own_table, 0, keepdims=False)
    narrow_weight = lax.dynamic_index_in_dim(narrow_projection, own_table, 0, keepdims=False)
    wide_rows = jnp.dot(wide_tables, wide_weight, preferred_element_type=jnp.float32)
    narrow_rows = jnp.dot(narrow_tables, narrow_weight, preferred_element_type=jnp.float32)

    wide_rows = pltpu.with_memory_space_constraint(wide_rows, pltpu.HBM)
    narrow_rows = pltpu.with_memory_space_constraint(narrow_rows, pltpu.HBM)
    keep, send, firsts, lists, blocks = pool_first(place, words, wide_rows, narrow_rows)
    both = added(keep, turned(send, "row", 2, 1))
    both, lists = lax.optimization_barrier((both, lists))
    moved = [
        turned(both[at * 512 : (at + 1) * 512], "x", 4, shift)
        for at, shift in enumerate(SHIFTS[:3])
    ]
    keep, send = pool_last(blocks, firsts, lists, wide_rows, narrow_rows)
    total = keep.astype(jnp.float32)
    for part in moved + [turned(send, "row", 2, 1)]:
        total = total + part.astype(jnp.float32)
    home = lax.all_to_all(
        total.astype(jnp.bfloat16).reshape(32, BAGS, 256), TABLES, 0, 0, tiled=True
    )

    bottom = dense_layer(
        dense_layer(dense_layer(dense_input, bottom_first), bottom_second), bottom_third
    )
    hidden, logits = top(bottom, home, top_first, top_last)
    return (hidden, logits.reshape(BAGS))


def solution(mesh):
    fine = Mesh(mesh.devices.reshape(4, 8, 4, 2), HOME)
    split = P(HOME)
    in_specs = (split, P(), P(), P()) + (split,) * 6 + (P(),) * 4
    return jax.shard_map(
        body, mesh=fine, in_specs=in_specs, out_specs=(split, split), check_vma=False
    )
```

```python
import jax
import jax.numpy as jnp
from jax import lax
from jax.experimental import pallas as pl
from jax.experimental.pallas import tpu as pltpu
from jax.sharding import Mesh
from jax.sharding import PartitionSpec as P

BAGS = 16
LANES = 128
ROWS = 4096
SOURCES = 256
LINES = 32
BLOCKS = 16
SHIFTS = (1, 3, 2, 0)
FEATURES = 65
PITCH = 72
INTER = 2208
TOP = 1024
SLABS = [pl.ds(0, 768), pl.ds(768, 768), pl.ds(1536, 672)]
LIMIT = pltpu.CompilerParams(vmem_limit_bytes=24 * 1024 * 1024)
VMEM = pl.BlockSpec(memory_space=pltpu.VMEM)
SMEM = pl.BlockSpec(memory_space=pltpu.SMEM)
ANY = pl.BlockSpec(memory_space=pl.ANY)
HBM = pl.BlockSpec(memory_space=pltpu.HBM)


def drawn_left(packed, field, unit, bits):
    for bit in range(bits):
        moved = jnp.where((packed & (1 << (field + bit))) != 0, packed, 0)
        packed = packed - moved + pltpu.roll(moved, LANES - (unit << bit), 1)
    return packed


def as_matrix(flags):
    return jnp.where(flags, 1.0, 0.0).astype(jnp.bfloat16)


def counted(flags, before):
    return jnp.dot(as_matrix(flags), before, preferred_element_type=jnp.float32).astype(jnp.int32)


def prepared(place_ref, words_ref, firsts_ref, more_v, lists_ref):
    my_x = place_ref[0]
    my_row = place_ref[1]
    shard = my_x * 2 + my_row
    at = lax.broadcasted_iota(jnp.int32, (LANES, LANES), 0)
    to = lax.broadcasted_iota(jnp.int32, (LANES, LANES), 1)
    same_bag = as_matrix(((at & 15) == (to & 15)) & (at < to))
    any_bag = as_matrix(at < to)
    lane = lax.broadcasted_iota(jnp.int32, (SOURCES, LANES), 1)
    target = lax.broadcasted_iota(jnp.int32, (SOURCES, LANES), 0) * BAGS + (lane & 15)
    parts = []
    for shift in SHIFTS:
        for row in (0, 1):
            start = ((my_x + shift) & 3) * 2 + (my_row ^ row)
            parts.append(words_ref[pl.ds(start, 32, stride=8), :])
    words = jnp.concatenate(parts, 0)
    most = jnp.int32(0)
    picks = []
    for kind, value in enumerate((words & 65535, (words >> 16) & 65535)):
        local = (value >> 12) == shard
        gap = (lane >> 4) - counted(local, same_bag)
        packed = jnp.where(local, (value & 4095) | (gap << 12) | (1 << 15), 0)
        packed = drawn_left(packed, 12, BAGS, 3)
        picks.append(jnp.where(packed != 0, packed & 4095, ROWS))
        more = (packed != 0) & (lane >= BAGS)
        before = counted(more, any_bag)
        most = jnp.maximum(most, jnp.max(before + more.astype(jnp.int32)))
        extra = (packed & 4095) | (target << 12) | ((lane - before) << 24) | jnp.int32(-(2**31))
        extra = drawn_left(jnp.where(more, extra, 0), 24, 1, 7)
        more_v[kind] = jnp.transpose(extra)
    pair = jnp.where(lane < BAGS, picks[0] | (picks[1] << 16), 0)
    for part in range(4):
        line = pair[part * 64 : part * 64 + 8]
        for j in range(1, 8):
            low = part * 64 + j * 8
            line = line + pltpu.roll(pair[low : low + 8], j * BAGS, 1)
        firsts_ref[part * 8 : (part + 1) * 8] = line
    lane = lax.broadcasted_iota(jnp.int32, (LINES, LANES), 1)

    def one_block(block, _):
        rows = pl.ds(pl.multiple_of(block * 8, 8), 8)
        held = jnp.concatenate(
            [
                more_v[kind, rows, half * LANES : (half + 1) * LANES]
                for kind in (0, 1)
                for half in (0, 1)
            ],
            0,
        )
        used = held < 0
        before = counted(used, any_bag)
        ones = used.astype(jnp.int32)
        total = jnp.sum(ones, axis=1, keepdims=True)
        part = jnp.sum(jnp.where(lane < 64, ones, 0), axis=1, keepdims=True)
        packed = jnp.where(used, (held & 0xFFFFFF) | ((lane - before) << 24), 0)
        packed = drawn_left(packed, 24, 1, 7) & 0xFFFFFF
        counts = jnp.where(lane == 0, total, 0) + jnp.where(lane == 1, part, 0)
        lists_ref[pl.ds(pl.multiple_of(block * LINES, LINES), LINES), :] = packed | (counts << 24)
        return 0

    blocks = jnp.maximum((most + 7) >> 3, 1)
    lax.fori_loop(0, blocks, one_block, 0)
    return blocks


def pooled(first_part, parts, blocks, first_line, firsts, lists_ref, lists, wide_rows, narrow_rows,
           wide_sum, narrow_sum, keep_ref, send_ref, sem):
    low_row = first_part * 1024
    spans = ((0, 0), (1, 1)) if parts == 3 else ((1, 2),)

    def block_copy(block):
        rows = pl.ds(pl.multiple_of(block * LINES, LINES), LINES)
        return pltpu.make_async_copy(lists_ref.at[rows], lists, sem)

    block_copy(0).start()

    def one_group(group, _):
        for part in range(parts):
            for j in range(8):
                base = pl.multiple_of(part * 1024 + j * 128 + group * BAGS, BAGS)
                for low in range(0, BAGS, 8):
                    bags = range(low, low + 8)
                    both = [firsts[first_line + part * 8 + group, j * BAGS + bag] for bag in bags]
                    wide = [wide_rows[pl.ds(pair & 65535, 1), :] for pair in both]
                    narrow = [narrow_rows[pl.ds(pair >> 16, 1), :] for pair in both]
                    for bag, row in zip(bags, wide):
                        wide_sum[pl.ds(base + bag, 1), :] = row
                    for bag, row in zip(bags, narrow):
                        narrow_sum[pl.ds(base + bag, 1), :] = row
        return 0

    lax.fori_loop(0, 8, one_group, 0)

    def one_block(block, _):
        @pl.when(block > 0)
        def _():
            block_copy(block).start()

        block_copy(block).wait()

        for kind, rows, sums in ((0, wide_rows, wide_sum), (1, narrow_rows, narrow_sum)):

            def some(k, low, count):
                entries = [lists[k, low + i] for i in range(count)]
                places = [pl.ds(((entry >> 12) & 4095) - low_row, 1) for entry in entries]
                values = [
                    sums[place, :] + rows[pl.ds(entry & 4095, 1), :]
                    for entry, place in zip(entries, places)
                ]
                for place, value in zip(places, values):
                    sums[place, :] = value

            for half, span in spans:

                def one_list(k, _, span=span):
                    low, high = 0, lax.shift_right_logical(lists[k, 0], 24)
                    if span:
                        middle = lax.shift_right_logical(lists[k, 1], 24)
                        low, high = (low, middle) if span == 1 else (middle, high)

                    def four(i, _):
                        some(k, low + i * 4, 4)
                        return 0

                    def one(i, _):
                        some(k, i, 1)
                        return 0

                    fours = (high - low) >> 2
                    lax.fori_loop(0, fours, four, 0)
                    lax.fori_loop(low + fours * 4, high, one, 0)
                    return 0

                start = kind * 16 + half * 8
                lax.fori_loop(start, start + 8, one_list, 0)
        return 0

    lax.fori_loop(0, blocks, one_block, 0)

    for part in range(parts):
        for row, ref in enumerate((keep_ref, send_ref)):

            def one(i, _):
                to = pl.ds(pl.multiple_of(part * 512 + i * 128, 128), 128)
                source = pl.ds(pl.multiple_of(part * 1024 + row * 512 + i * 128, 128), 128)
                ref[to, 0:LANES] = wide_sum[source, :].astype(jnp.bfloat16)
                ref[to, LANES:] = narrow_sum[source, :].astype(jnp.bfloat16)
                return 0

            lax.fori_loop(0, 4, one, 0)


def table_copies(wide_ref, narrow_ref, wide_rows, narrow_rows, sems):
    pairs = ((wide_ref, wide_rows), (narrow_ref, narrow_rows))
    copies = []
    for at, (ref, rows) in enumerate(pairs):
        copies.append(pltpu.make_async_copy(ref, rows.at[pl.ds(0, ROWS)], sems.at[at]))
        copies[-1].start()
        rows[pl.ds(ROWS, 8), :] = jnp.zeros((8, LANES), jnp.float32)
    return copies


def first_kernel(place_ref, words_ref, wide_ref, narrow_ref, keep_ref, send_ref, firsts_ref,
                 lists_ref, blocks_ref, more_v, wide_rows, narrow_rows, wide_sum, narrow_sum,
                 firsts, lists, sems):
    copies = table_copies(wide_ref, narrow_ref, wide_rows, narrow_rows, sems)
    blocks = prepared(place_ref, words_ref, firsts_ref, more_v, lists_ref)
    blocks_ref[0] = blocks
    copies.append(pltpu.make_async_copy(firsts_ref, firsts, sems.at[2]))
    copies[-1].start()
    for copy in copies:
        copy.wait()
    pooled(0, 3, blocks, 0, firsts, lists_ref, lists, wide_rows, narrow_rows, wide_sum, narrow_sum,
           keep_ref, send_ref, sems.at[3])


def last_kernel(blocks_ref, firsts_ref, lists_ref, wide_ref, narrow_ref, keep_ref, send_ref,
                wide_rows, narrow_rows, wide_sum, narrow_sum, lists, sems):
    copies = table_copies(wide_ref, narrow_ref, wide_rows, narrow_rows, sems)
    for copy in copies:
        copy.wait()
    pooled(3, 1, blocks_ref[0], 24, firsts_ref, lists_ref, lists, wide_rows, narrow_rows, wide_sum,
           narrow_sum, keep_ref, send_ref, sems.at[2])


def shapes(parts):
    half = jax.ShapeDtypeStruct((parts * 512, 2 * LANES), jnp.bfloat16)
    rows = pltpu.VMEM((ROWS + 8, LANES), jnp.float32)
    sums = pltpu.VMEM((parts * 1024, LANES), jnp.float32)
    cost = pl.CostEstimate(flops=10**6, bytes_accessed=10**7, transcendentals=0)
    return half, [rows, rows, sums, sums], cost


def pool_first(place, words, wide, narrow):
    half, buffers, cost = shapes(3)
    return pl.pallas_call(
        first_kernel,
        out_shape=(
            half,
            half,
            jax.ShapeDtypeStruct((32, LANES), jnp.int32),
            jax.ShapeDtypeStruct((BLOCKS * LINES, LANES), jnp.int32),
            jax.ShapeDtypeStruct((1,), jnp.int32),
        ),
        in_specs=[SMEM, VMEM, HBM, HBM],
        out_specs=(VMEM, VMEM, VMEM, VMEM, SMEM),
        scratch_shapes=[pltpu.VMEM((2, LANES, SOURCES), jnp.int32)]
        + buffers
        + [
            pltpu.SMEM((LINES, LANES), jnp.int32),
            pltpu.SMEM((LINES, LANES), jnp.int32),
            pltpu.SemaphoreType.DMA((4,)),
        ],
        compiler_params=LIMIT,
        cost_estimate=cost,
        name="pool_first",
    )(place, words, wide, narrow)


def pool_last(blocks, firsts, lists, wide, narrow):
    half, buffers, cost = shapes(1)
    return pl.pallas_call(
        last_kernel,
        out_shape=(half, half),
        in_specs=[SMEM, SMEM, ANY, HBM, HBM],
        out_specs=(VMEM, VMEM),
        scratch_shapes=buffers
        + [pltpu.SMEM((LINES, LANES), jnp.int32), pltpu.SemaphoreType.DMA((3,))],
        compiler_params=LIMIT,
        cost_estimate=cost,
        name="pool_last",
    )(blocks, firsts, lists, wide, narrow)


def top_kernel(bottom_ref, home_ref, first_ref, last_ref, hidden_ref, logits_ref, stack, grams, joined,
               first, sems):
    copies = []
    for at, rows in enumerate(SLABS):
        copies.append(pltpu.make_async_copy(first_ref.at[rows], first.at[rows], sems.at[at]))
        copies[-1].start()
    bottom = bottom_ref[...].astype(jnp.float32)
    stack[:, 0:1, :] = bottom[:, None, :]
    for table in range(32):
        both = home_ref[table].astype(jnp.float32)
        stack[:, 1 + table : 2 + table, :] = both[:, None, :LANES]
        stack[:, 33 + table : 34 + table, :] = both[:, None, LANES:]
    stack[:, FEATURES:, :] = jnp.zeros((BAGS, PITCH - FEATURES, LANES), jnp.float32)
    for bag in range(BAGS):
        features = stack[bag].astype(jnp.bfloat16)
        grams[bag * PITCH : (bag + 1) * PITCH, 0:PITCH] = lax.dot_general(
            features, features, (((1,), (1,)), ((), ())), preferred_element_type=jnp.float32
        )
    joined[:, 0:LANES] = bottom
    at = LANES
    for f in range(FEATURES - 1):
        count = FEATURES - 1 - f
        line = grams[pl.ds(f, BAGS, stride=PITCH), :]
        joined[:, at : at + count] = line[:, f + 1 : FEATURES]
        at += count
    hidden = jnp.zeros((BAGS, TOP), jnp.float32)
    for copy, rows in zip(copies, SLABS):
        copy.wait()
        hidden = hidden + jnp.dot(
            joined[:, rows].astype(jnp.bfloat16), first[rows, :], preferred_element_type=jnp.float32
        )
    hidden = jnp.maximum(hidden, 0.0).astype(jnp.bfloat16)
    hidden_ref[...] = hidden
    logits_ref[...] = lax.dot_general(
        last_ref[...], hidden, (((1,), (1,)), ((), ())), preferred_element_type=jnp.float32
    )


def top(bottom, home, top_first, top_last):
    return pl.pallas_call(
        top_kernel,
        out_shape=(
            jax.ShapeDtypeStruct((BAGS, TOP), jnp.bfloat16),
            jax.ShapeDtypeStruct((1, BAGS), jnp.float32),
        ),
        in_specs=[VMEM, VMEM, HBM, VMEM],
        out_specs=(VMEM, VMEM),
        scratch_shapes=[
            pltpu.VMEM((BAGS, PITCH, LANES), jnp.float32),
            pltpu.VMEM((BAGS * PITCH, LANES), jnp.float32),
            pltpu.VMEM((BAGS, INTER), jnp.float32),
            pltpu.VMEM((INTER, TOP), jnp.bfloat16),
            pltpu.SemaphoreType.DMA((3,)),
        ],
        compiler_params=pltpu.CompilerParams(vmem_limit_bytes=16 * 1024 * 1024),
        name="top",
    )(bottom, home, top_first, top_last.reshape(1, TOP))


HOME = ("y", "z", "x", "row")
TABLES = ("y", "z")


def dense_layer(values, weight):
    return jnp.maximum(jnp.dot(values, weight, preferred_element_type=jnp.float32), 0.0).astype(
        jnp.bfloat16
    )


def turned(block, axis, count, shift):
    return lax.ppermute(block, axis, [(i, (i + shift) % count) for i in range(count)])


def added(one, other):
    return (one.astype(jnp.float32) + other.astype(jnp.float32)).astype(jnp.bfloat16)


def coded(indices, lengths):
    slots = lax.broadcasted_iota(jnp.int32, indices.shape, 2)
    return jnp.where(slots < lengths[:, :, None], indices, 32768)


def body(
    dense_input,
    bottom_first,
    bottom_second,
    bottom_third,
    wide_tables,
    narrow_tables,
    wide_indices,
    wide_lengths,
    narrow_indices,
    narrow_lengths,
    wide_projection,
    narrow_projection,
    top_first,
    top_last,
):
    own_table = lax.axis_index(TABLES)
    place = jnp.stack([lax.axis_index("x"), lax.axis_index("row")]).astype(jnp.int32)

    words = coded(wide_indices, wide_lengths) | (coded(narrow_indices, narrow_lengths) << 16)
    words = jnp.transpose(words, (1, 2, 0)).reshape(32, 1, LANES)
    words = jnp.broadcast_to(words, (32, 8, LANES)).reshape(256, LANES)
    words = lax.all_to_all(words, HOME, 0, 0, tiled=True)

    wide_weight = lax.dynamic_index_in_dim(wide_projection, own_table, 0, keepdims=False)
    narrow_weight = lax.dynamic_index_in_dim(narrow_projection, own_table, 0, keepdims=False)
    wide_rows = jnp.dot(wide_tables, wide_weight, preferred_element_type=jnp.float32)
    narrow_rows = jnp.dot(narrow_tables, narrow_weight, preferred_element_type=jnp.float32)

    wide_rows = pltpu.with_memory_space_constraint(wide_rows, pltpu.HBM)
    narrow_rows = pltpu.with_memory_space_constraint(narrow_rows, pltpu.HBM)
    keep, send, firsts, lists, blocks = pool_first(place, words, wide_rows, narrow_rows)
    both = added(keep, turned(send, "row", 2, 1))
    both, lists = lax.optimization_barrier((both, lists))
    moved = [
        turned(both[at * 512 : (at + 1) * 512], "x", 4, shift)
        for at, shift in enumerate(SHIFTS[:3])
    ]
    keep, send = pool_last(blocks, firsts, lists, wide_rows, narrow_rows)
    total = keep.astype(jnp.float32)
    for part in moved + [turned(send, "row", 2, 1)]:
        total = total + part.astype(jnp.float32)
    home = lax.all_to_all(
        total.astype(jnp.bfloat16).reshape(32, BAGS, 256), TABLES, 0, 0, tiled=True
    )

    bottom = dense_layer(
        dense_layer(dense_layer(dense_input, bottom_first), bottom_second), bottom_third
    )
    top_first = pltpu.with_memory_space_constraint(top_first, pltpu.HBM)
    hidden, logits = top(bottom, home, top_first, top_last)
    return (hidden, logits.reshape(BAGS))


def solution(mesh):
    fine = Mesh(mesh.devices.reshape(4, 8, 4, 2), HOME)
    split = P(HOME)
    in_specs = (split, P(), P(), P()) + (split,) * 6 + (P(),) * 4
    return jax.shard_map(
        body, mesh=fine, in_specs=in_specs, out_specs=(split, split), check_vma=False
    )
```

```python
import jax
import jax.numpy as jnp
from jax import lax
from jax.experimental import pallas as pl
from jax.experimental.pallas import tpu as pltpu
from jax.sharding import Mesh
from jax.sharding import PartitionSpec as P

BAGS = 16
LANES = 128
ROWS = 4096
SOURCES = 256
LINES = 32
BLOCKS = 16
SHIFTS = (1, 3, 2, 0)
FEATURES = 65
PITCH = 72
INTER = 2208
TOP = 1024
SLABS = [pl.ds(at, min(256, INTER - at)) for at in range(0, INTER, 256)]
LIMIT = pltpu.CompilerParams(vmem_limit_bytes=24 * 1024 * 1024)
VMEM = pl.BlockSpec(memory_space=pltpu.VMEM)
SMEM = pl.BlockSpec(memory_space=pltpu.SMEM)
ANY = pl.BlockSpec(memory_space=pl.ANY)
HBM = pl.BlockSpec(memory_space=pltpu.HBM)


def drawn_left(packed, field, unit, bits):
    for bit in range(bits):
        moved = jnp.where((packed & (1 << (field + bit))) != 0, packed, 0)
        packed = packed - moved + pltpu.roll(moved, LANES - (unit << bit), 1)
    return packed


def as_matrix(flags):
    return jnp.where(flags, 1.0, 0.0).astype(jnp.bfloat16)


def counted(flags, before):
    return jnp.dot(as_matrix(flags), before, preferred_element_type=jnp.float32).astype(jnp.int32)


def prepared(place_ref, words_ref, firsts_ref, more_v, lists_ref):
    my_x = place_ref[0]
    my_row = place_ref[1]
    shard = my_x * 2 + my_row
    at = lax.broadcasted_iota(jnp.int32, (LANES, LANES), 0)
    to = lax.broadcasted_iota(jnp.int32, (LANES, LANES), 1)
    same_bag = as_matrix(((at & 15) == (to & 15)) & (at < to))
    any_bag = as_matrix(at < to)
    lane = lax.broadcasted_iota(jnp.int32, (SOURCES, LANES), 1)
    target = lax.broadcasted_iota(jnp.int32, (SOURCES, LANES), 0) * BAGS + (lane & 15)
    parts = []
    for shift in SHIFTS:
        for row in (0, 1):
            start = ((my_x + shift) & 3) * 2 + (my_row ^ row)
            parts.append(words_ref[pl.ds(start, 32, stride=8), :])
    words = jnp.concatenate(parts, 0)
    most = jnp.int32(0)
    picks = []
    for kind, value in enumerate((words & 65535, (words >> 16) & 65535)):
        local = (value >> 12) == shard
        gap = (lane >> 4) - counted(local, same_bag)
        packed = jnp.where(local, (value & 4095) | (gap << 12) | (1 << 15), 0)
        packed = drawn_left(packed, 12, BAGS, 3)
        picks.append(jnp.where(packed != 0, packed & 4095, ROWS))
        more = (packed != 0) & (lane >= BAGS)
        before = counted(more, any_bag)
        most = jnp.maximum(most, jnp.max(before + more.astype(jnp.int32)))
        extra = (packed & 4095) | (target << 12) | ((lane - before) << 24) | jnp.int32(-(2**31))
        extra = drawn_left(jnp.where(more, extra, 0), 24, 1, 7)
        more_v[kind] = jnp.transpose(extra)
    pair = jnp.where(lane < BAGS, picks[0] | (picks[1] << 16), 0)
    for part in range(4):
        line = pair[part * 64 : part * 64 + 8]
        for j in range(1, 8):
            low = part * 64 + j * 8
            line = line + pltpu.roll(pair[low : low + 8], j * BAGS, 1)
        firsts_ref[part * 8 : (part + 1) * 8] = line
    lane = lax.broadcasted_iota(jnp.int32, (LINES, LANES), 1)

    def one_block(block, _):
        rows = pl.ds(pl.multiple_of(block * 8, 8), 8)
        held = jnp.concatenate(
            [
                more_v[kind, rows, half * LANES : (half + 1) * LANES]
                for kind in (0, 1)
                for half in (0, 1)
            ],
            0,
        )
        used = held < 0
        before = counted(used, any_bag)
        ones = used.astype(jnp.int32)
        total = jnp.sum(ones, axis=1, keepdims=True)
        part = jnp.sum(jnp.where(lane < 64, ones, 0), axis=1, keepdims=True)
        packed = jnp.where(used, (held & 0xFFFFFF) | ((lane - before) << 24), 0)
        packed = drawn_left(packed, 24, 1, 7) & 0xFFFFFF
        counts = jnp.where(lane == 0, total, 0) + jnp.where(lane == 1, part, 0)
        lists_ref[pl.ds(pl.multiple_of(block * LINES, LINES), LINES), :] = packed | (counts << 24)
        return 0

    blocks = jnp.maximum((most + 7) >> 3, 1)
    lax.fori_loop(0, blocks, one_block, 0)
    return blocks


def pooled(first_part, parts, blocks, first_line, firsts, lists_ref, lists, wide_rows, narrow_rows,
           wide_sum, narrow_sum, keep_ref, send_ref, sem):
    low_row = first_part * 1024
    spans = ((0, 0), (1, 1)) if parts == 3 else ((1, 2),)

    def block_copy(block):
        rows = pl.ds(pl.multiple_of(block * LINES, LINES), LINES)
        return pltpu.make_async_copy(lists_ref.at[rows], lists, sem)

    block_copy(0).start()

    def one_group(group, _):
        for part in range(parts):
            for j in range(8):
                base = pl.multiple_of(part * 1024 + j * 128 + group * BAGS, BAGS)
                for low in range(0, BAGS, 8):
                    bags = range(low, low + 8)
                    both = [firsts[first_line + part * 8 + group, j * BAGS + bag] for bag in bags]
                    wide = [wide_rows[pl.ds(pair & 65535, 1), :] for pair in both]
                    narrow = [narrow_rows[pl.ds(pair >> 16, 1), :] for pair in both]
                    for bag, row in zip(bags, wide):
                        wide_sum[pl.ds(base + bag, 1), :] = row
                    for bag, row in zip(bags, narrow):
                        narrow_sum[pl.ds(base + bag, 1), :] = row
        return 0

    lax.fori_loop(0, 8, one_group, 0)

    def one_block(block, _):
        @pl.when(block > 0)
        def _():
            block_copy(block).start()

        block_copy(block).wait()

        for kind, rows, sums in ((0, wide_rows, wide_sum), (1, narrow_rows, narrow_sum)):

            def some(k, low, count):
                entries = [lists[k, low + i] for i in range(count)]
                places = [pl.ds(((entry >> 12) & 4095) - low_row, 1) for entry in entries]
                values = [
                    sums[place, :] + rows[pl.ds(entry & 4095, 1), :]
                    for entry, place in zip(entries, places)
                ]
                for place, value in zip(places, values):
                    sums[place, :] = value

            for half, span in spans:

                def one_list(k, _, span=span):
                    low, high = 0, lax.shift_right_logical(lists[k, 0], 24)
                    if span:
                        middle = lax.shift_right_logical(lists[k, 1], 24)
                        low, high = (low, middle) if span == 1 else (middle, high)

                    def four(i, _):
                        some(k, low + i * 4, 4)
                        return 0

                    def one(i, _):
                        some(k, i, 1)
                        return 0

                    fours = (high - low) >> 2
                    lax.fori_loop(0, fours, four, 0)
                    lax.fori_loop(low + fours * 4, high, one, 0)
                    return 0

                start = kind * 16 + half * 8
                lax.fori_loop(start, start + 8, one_list, 0)
        return 0

    lax.fori_loop(0, blocks, one_block, 0)

    for part in range(parts):
        for row, ref in enumerate((keep_ref, send_ref)):

            def one(i, _):
                to = pl.ds(pl.multiple_of(part * 512 + i * 128, 128), 128)
                source = pl.ds(pl.multiple_of(part * 1024 + row * 512 + i * 128, 128), 128)
                ref[to, 0:LANES] = wide_sum[source, :].astype(jnp.bfloat16)
                ref[to, LANES:] = narrow_sum[source, :].astype(jnp.bfloat16)
                return 0

            lax.fori_loop(0, 4, one, 0)


def table_copies(wide_ref, narrow_ref, wide_rows, narrow_rows, sems):
    pairs = ((wide_ref, wide_rows), (narrow_ref, narrow_rows))
    copies = []
    for at, (ref, rows) in enumerate(pairs):
        copies.append(pltpu.make_async_copy(ref, rows.at[pl.ds(0, ROWS)], sems.at[at]))
        copies[-1].start()
        rows[pl.ds(ROWS, 8), :] = jnp.zeros((8, LANES), jnp.float32)
    return copies


def first_kernel(place_ref, words_ref, wide_ref, narrow_ref, keep_ref, send_ref, firsts_ref,
                 lists_ref, blocks_ref, more_v, wide_rows, narrow_rows, wide_sum, narrow_sum,
                 firsts, lists, sems):
    copies = table_copies(wide_ref, narrow_ref, wide_rows, narrow_rows, sems)
    blocks = prepared(place_ref, words_ref, firsts_ref, more_v, lists_ref)
    blocks_ref[0] = blocks
    copies.append(pltpu.make_async_copy(firsts_ref, firsts, sems.at[2]))
    copies[-1].start()
    for copy in copies:
        copy.wait()
    pooled(0, 3, blocks, 0, firsts, lists_ref, lists, wide_rows, narrow_rows, wide_sum, narrow_sum,
           keep_ref, send_ref, sems.at[3])


def last_kernel(blocks_ref, firsts_ref, lists_ref, wide_ref, narrow_ref, keep_ref, send_ref,
                wide_rows, narrow_rows, wide_sum, narrow_sum, lists, sems):
    copies = table_copies(wide_ref, narrow_ref, wide_rows, narrow_rows, sems)
    for copy in copies:
        copy.wait()
    pooled(3, 1, blocks_ref[0], 24, firsts_ref, lists_ref, lists, wide_rows, narrow_rows, wide_sum,
           narrow_sum, keep_ref, send_ref, sems.at[2])


def shapes(parts):
    half = jax.ShapeDtypeStruct((parts * 512, 2 * LANES), jnp.bfloat16)
    rows = pltpu.VMEM((ROWS + 8, LANES), jnp.float32)
    sums = pltpu.VMEM((parts * 1024, LANES), jnp.float32)
    cost = pl.CostEstimate(flops=10**6, bytes_accessed=10**7, transcendentals=0)
    return half, [rows, rows, sums, sums], cost


def pool_first(place, words, wide, narrow):
    half, buffers, cost = shapes(3)
    return pl.pallas_call(
        first_kernel,
        out_shape=(
            half,
            half,
            jax.ShapeDtypeStruct((32, LANES), jnp.int32),
            jax.ShapeDtypeStruct((BLOCKS * LINES, LANES), jnp.int32),
            jax.ShapeDtypeStruct((1,), jnp.int32),
        ),
        in_specs=[SMEM, VMEM, HBM, HBM],
        out_specs=(VMEM, VMEM, VMEM, VMEM, SMEM),
        scratch_shapes=[pltpu.VMEM((2, LANES, SOURCES), jnp.int32)]
        + buffers
        + [
            pltpu.SMEM((LINES, LANES), jnp.int32),
            pltpu.SMEM((LINES, LANES), jnp.int32),
            pltpu.SemaphoreType.DMA((4,)),
        ],
        compiler_params=LIMIT,
        cost_estimate=cost,
        name="pool_first",
    )(place, words, wide, narrow)


def pool_last(blocks, firsts, lists, wide, narrow):
    half, buffers, cost = shapes(1)
    return pl.pallas_call(
        last_kernel,
        out_shape=(half, half),
        in_specs=[SMEM, SMEM, ANY, HBM, HBM],
        out_specs=(VMEM, VMEM),
        scratch_shapes=buffers
        + [pltpu.SMEM((LINES, LANES), jnp.int32), pltpu.SemaphoreType.DMA((3,))],
        compiler_params=LIMIT,
        cost_estimate=cost,
        name="pool_last",
    )(blocks, firsts, lists, wide, narrow)


def top_kernel(bottom_ref, home_ref, first_ref, last_ref, hidden_ref, logits_ref, stack, grams, joined,
               first, sems):
    copies = []
    for at, rows in enumerate(SLABS):
        copies.append(pltpu.make_async_copy(first_ref.at[rows], first.at[rows], sems.at[at]))
        copies[-1].start()
    bottom = bottom_ref[...].astype(jnp.float32)
    stack[:, 0:1, :] = bottom[:, None, :]
    for table in range(32):
        both = home_ref[table].astype(jnp.float32)
        stack[:, 1 + table : 2 + table, :] = both[:, None, :LANES]
        stack[:, 33 + table : 34 + table, :] = both[:, None, LANES:]
    stack[:, FEATURES:, :] = jnp.zeros((BAGS, PITCH - FEATURES, LANES), jnp.float32)
    for bag in range(BAGS):
        features = stack[bag].astype(jnp.bfloat16)
        grams[bag * PITCH : (bag + 1) * PITCH, 0:PITCH] = lax.dot_general(
            features, features, (((1,), (1,)), ((), ())), preferred_element_type=jnp.float32
        )
    joined[:, 0:LANES] = bottom
    at = LANES
    for f in range(FEATURES - 1):
        count = FEATURES - 1 - f
        line = grams[pl.ds(f, BAGS, stride=PITCH), :]
        joined[:, at : at + count] = line[:, f + 1 : FEATURES]
        at += count
    hidden = jnp.zeros((BAGS, TOP), jnp.float32)
    for copy, rows in zip(copies, SLABS):
        copy.wait()
        hidden = hidden + jnp.dot(
            joined[:, rows].astype(jnp.bfloat16), first[rows, :], preferred_element_type=jnp.float32
        )
    hidden = jnp.maximum(hidden, 0.0).astype(jnp.bfloat16)
    hidden_ref[...] = hidden
    logits_ref[...] = lax.dot_general(
        last_ref[...], hidden, (((1,), (1,)), ((), ())), preferred_element_type=jnp.float32
    )


def top(bottom, home, top_first, top_last):
    return pl.pallas_call(
        top_kernel,
        out_shape=(
            jax.ShapeDtypeStruct((BAGS, TOP), jnp.bfloat16),
            jax.ShapeDtypeStruct((1, BAGS), jnp.float32),
        ),
        in_specs=[VMEM, VMEM, HBM, VMEM],
        out_specs=(VMEM, VMEM),
        scratch_shapes=[
            pltpu.VMEM((BAGS, PITCH, LANES), jnp.float32),
            pltpu.VMEM((BAGS * PITCH, LANES), jnp.float32),
            pltpu.VMEM((BAGS, INTER), jnp.float32),
            pltpu.VMEM((INTER, TOP), jnp.bfloat16),
            pltpu.SemaphoreType.DMA((len(SLABS),)),
        ],
        compiler_params=pltpu.CompilerParams(vmem_limit_bytes=16 * 1024 * 1024),
        name="top",
    )(bottom, home, top_first, top_last.reshape(1, TOP))


HOME = ("y", "z", "x", "row")
TABLES = ("y", "z")


def dense_layer(values, weight):
    return jnp.maximum(jnp.dot(values, weight, preferred_element_type=jnp.float32), 0.0).astype(
        jnp.bfloat16
    )


def turned(block, axis, count, shift):
    return lax.ppermute(block, axis, [(i, (i + shift) % count) for i in range(count)])


def added(one, other):
    return (one.astype(jnp.float32) + other.astype(jnp.float32)).astype(jnp.bfloat16)


def coded(indices, lengths):
    slots = lax.broadcasted_iota(jnp.int32, indices.shape, 2)
    return jnp.where(slots < lengths[:, :, None], indices, 32768)


def body(
    dense_input,
    bottom_first,
    bottom_second,
    bottom_third,
    wide_tables,
    narrow_tables,
    wide_indices,
    wide_lengths,
    narrow_indices,
    narrow_lengths,
    wide_projection,
    narrow_projection,
    top_first,
    top_last,
):
    own_table = lax.axis_index(TABLES)
    place = jnp.stack([lax.axis_index("x"), lax.axis_index("row")]).astype(jnp.int32)

    words = coded(wide_indices, wide_lengths) | (coded(narrow_indices, narrow_lengths) << 16)
    words = jnp.transpose(words, (1, 2, 0)).reshape(32, 1, LANES)
    words = jnp.broadcast_to(words, (32, 8, LANES)).reshape(256, LANES)
    words = lax.all_to_all(words, HOME, 0, 0, tiled=True)

    wide_weight = lax.dynamic_index_in_dim(wide_projection, own_table, 0, keepdims=False)
    narrow_weight = lax.dynamic_index_in_dim(narrow_projection, own_table, 0, keepdims=False)
    wide_rows = jnp.dot(wide_tables, wide_weight, preferred_element_type=jnp.float32)
    narrow_rows = jnp.dot(narrow_tables, narrow_weight, preferred_element_type=jnp.float32)

    wide_rows = pltpu.with_memory_space_constraint(wide_rows, pltpu.HBM)
    narrow_rows = pltpu.with_memory_space_constraint(narrow_rows, pltpu.HBM)
    keep, send, firsts, lists, blocks = pool_first(place, words, wide_rows, narrow_rows)
    both = added(keep, turned(send, "row", 2, 1))
    both, lists = lax.optimization_barrier((both, lists))
    moved = [
        turned(both[at * 512 : (at + 1) * 512], "x", 4, shift)
        for at, shift in enumerate(SHIFTS[:3])
    ]
    keep, send = pool_last(blocks, firsts, lists, wide_rows, narrow_rows)
    total = keep.astype(jnp.float32)
    for part in moved + [turned(send, "row", 2, 1)]:
        total = total + part.astype(jnp.float32)
    home = lax.all_to_all(
        total.astype(jnp.bfloat16).reshape(32, BAGS, 256), TABLES, 0, 0, tiled=True
    )

    bottom = dense_layer(
        dense_layer(dense_layer(dense_input, bottom_first), bottom_second), bottom_third
    )
    top_first = pltpu.with_memory_space_constraint(top_first, pltpu.HBM)
    hidden, logits = top(bottom, home, top_first, top_last)
    return (hidden, logits.reshape(BAGS))


def solution(mesh):
    fine = Mesh(mesh.devices.reshape(4, 8, 4, 2), HOME)
    split = P(HOME)
    in_specs = (split, P(), P(), P()) + (split,) * 6 + (P(),) * 4
    return jax.shard_map(
        body, mesh=fine, in_specs=in_specs, out_specs=(split, split), check_vma=False
    )
```
